32 devices in a mesh: dp: 8 (over y, x, core), expert: 4 (over z).
Axes of the slice: x: 2, y: 2, z: 4, core: 2. Of those that a mesh axis runs over, the one named last changes fastest.
Arguments:
- tokens: bfloat16 [2048, 1024], P(('dp', 'expert')), may hold values from -6 to 6
- expert_ids: int32 [2048, 2], P(('dp', 'expert')), may hold values from 0 to 7, all different within a row; in each aligned block of 64 rows (0 to 63, 64 to 127, ...) at most 20 rows name the same one
- gate_weights: float32 [2048, 2], P(('dp', 'expert')), may hold values from 0.2 to 1
- w_gate: bfloat16 [8, 1024, 4096], P('expert', None, 'dp'), may hold values from -0.1875 to 0.1875
- w_up: bfloat16 [8, 1024, 4096], P('expert', None, 'dp'), may hold values from -0.1875 to 0.1875
- w_down: bfloat16 [8, 4096, 1024], P('expert', 'dp'), may hold values from -0.09375 to 0.09375
- cotangent: bfloat16 [2048, 1024], P(('dp', 'expert')), may hold values from -6 to 6
Outputs:
- mixed: bfloat16 [2048, 1024], P(('dp', 'expert'))
- grad_tokens: bfloat16 [2048, 1024], P(('dp', 'expert'))
- grad_gate: bfloat16 [8, 1024, 4096], P('expert', None, 'dp')
- grad_up: bfloat16 [8, 1024, 4096], P('expert', None, 'dp')
- grad_down: bfloat16 [8, 4096, 1024], P('expert', 'dp')
The draws below stay inside these ranges and needn't reach their ends.
Inputs may be any that keep to these rules, and one draw needn't show every extreme that they name: `expert_ids`: in every aligned block of 64 rows (the rows of one device) no expert is named more than 20 times, a bound that some block reaches; the 2 experts of a row differ.
All inputs are finite; a program needn't handle non-finite values.
Results may differ from the reference program's by a relative error of at most 0.019.
Values may be sent and summed in bfloat16 or wider, within the bound.
No kernel may reach another device: no remote copies, remote signals or barrier semaphores. Data moves between devices by JAX's collectives and lax.ppermute only.
A program may use at most 192 MiB of HBM per device.

```python
import math
import jax
import jax.numpy as jnp
import numpy as np
from jax import lax

D = 1024
FF = 4096
EXPERTS = 8
TOP = 2
TOK_DEV = 64
CAP = 20
TOKENS = 2048
N_DP = 8


def steps_of(key, dims, split, smallest, top_value):
    level, own = 1.0, jax.random.fold_in(key, 6)
    for dim, blocks in split:
        heights = jnp.exp(jax.random.uniform(jax.random.fold_in(own, dim), (blocks,), jnp.float32, smallest / len(split), top_value / len(split)))
        level = level * jnp.repeat(heights, dims[dim] // blocks).reshape([-1 if axis == dim else 1 for axis in range(len(dims))])
    return level


def deal_out(own_key, own, number, rows, number_of, top, most, slope):
    sequence = jax.random.permutation(own_key, number_of)
    crowded, common = portions_of(number_of, rows * top, most, slope, True), portions_of(number_of, rows * top, most, slope, False)
    places = jnp.arange(number_of)

    def named(tallies, offset_by):
        used = int((tallies > 0).sum())
        fixed = max(1, used // 4)
        shifted = fixed + (places - fixed + offset_by * (used - fixed)) % max(1, number_of - fixed)
        return jnp.zeros((number_of,), jnp.int32).at[sequence[jnp.where(places < fixed, places, shifted)]].set(jnp.asarray(tallies, jnp.int32))

    tallies = jnp.where(number % 4 == 0, named(crowded, number // 4), named(common, number - number // 4 - 1))
    mixed = jax.random.permutation(jax.random.fold_in(own, 3), number_of)
    donor, taker = mixed[0:number_of // 2 * 2:2], mixed[1:number_of // 2 * 2:2]
    margin = jnp.minimum(tallies[donor] - 1, most - tallies[taker]) // 2
    margin = jnp.where((donor == sequence[0]) | (taker == sequence[0]) | (tallies[taker] == 0), 0, jnp.maximum(margin, 0))
    shifted = jax.random.randint(jax.random.fold_in(own, 4), (number_of // 2,), 0, 1 << 20) % (margin + 1)
    tallies = tallies.at[donor].add(-shifted).at[taker].add(shifted)
    labels = jnp.searchsorted(jnp.cumsum(tallies), jnp.arange(rows * top), side="right").astype(jnp.int32)
    table = labels.reshape(top, rows).T
    table = table[jax.random.permutation(jax.random.fold_in(own, 1), rows)]
    offset_by = jax.random.randint(jax.random.fold_in(own, 2), (rows, 1), 0, top)
    return jnp.take_along_axis(table, (jnp.arange(top)[None, :] + offset_by) % top, axis=1)


def portions_of(count, total, bound, lean, full):
    weights = [(1 << 20) // math.isqrt(standing ** lean) + 1 for standing in range(1, count + 1)]
    largest = bound if full else min(bound, max(-(-total // count), total * weights[0] // sum(weights)))
    least = 1 if total - largest >= count - 1 else 0
    counts, surplus = [largest] + [least] * (count - 1), total - largest - least * (count - 1)
    while surplus > 0:
        free = [i for i in range(1, count) if counts[i] < largest] or [i for i in range(1, count) if counts[i] < bound]
        mass, left = sum([weights[i] for i in free]), surplus
        for i in free:
            addition = min(bound - counts[i], max(1, left * weights[i] // mass), surplus)
            counts[i] = counts[i] + addition
            surplus = surplus - addition
    return np.array(counts)


def bell_draw(own_key, shape, deviation, reach, pieces=(), held_as=jnp.bfloat16):
    array = jax.random.normal(own_key, shape, jnp.float32) * deviation
    if len(pieces) > 0:
        array = steps_of(own_key, shape, pieces, -0.22, 0.18) * array
    return jnp.clip(array, min=-reach, max=reach).astype(held_as)


def setup_inputs(seed: int = 0) -> dict:
    keys = jax.random.split(jax.random.key(seed), 8)
    tokens = bell_draw(keys[0], (TOKENS, D), 1.0, 6.0, ((0, 32),))
    expert_ids_keys = jax.random.split(jax.random.fold_in(keys[1], 1), TOKENS // TOK_DEV)
    expert_ids_turns = jax.random.permutation(jax.random.fold_in(keys[1], 3), TOKENS // TOK_DEV)
    expert_ids = jax.vmap(lambda own, number: deal_out(jax.random.fold_in(keys[1], 2), own, number, TOK_DEV, EXPERTS, TOP, CAP, 2))(expert_ids_keys, expert_ids_turns).reshape((TOKENS, TOP))
    gate_weights = jnp.clip(0.2 + 0.8 * jax.random.uniform(keys[2], (TOKENS, TOP), jnp.float32) ** steps_of(keys[2], (TOKENS, TOP), ((0, 32),), -0.2, 0.2), 0.2, 1.0)
    w_gate = bell_draw(keys[3], (EXPERTS, D, FF), D ** -0.5, 0.1875, ((0, 4), (2, 8)))
    w_up = bell_draw(keys[4], (EXPERTS, D, FF), D ** -0.5, 0.1875, ((0, 4), (2, 8)))
    w_down = bell_draw(keys[5], (EXPERTS, FF, D), FF ** -0.5, 0.09375, ((0, 4), (1, 8)))
    cotangent = bell_draw(keys[6], (TOKENS, D), 1.0, 6.0, ((0, 32),))
    return dict(tokens=tokens, expert_ids=expert_ids, gate_weights=gate_weights, w_gate=w_gate, w_up=w_up, w_down=w_down, cotangent=cotangent)


def round_groups(parts):
    rounded = lax.optimization_barrier(parts.astype(jnp.bfloat16))
    return jnp.sum(rounded.astype(jnp.float32), axis=0).astype(jnp.bfloat16)


def expert_pass(operands):
    x_rows, dy_rows, wg, wu, wd = operands
    fpart = FF // N_DP
    count = x_rows.shape[0]
    gate = jnp.dot(x_rows, wg, preferred_element_type=jnp.float32)
    up = jnp.dot(x_rows, wu, preferred_element_type=jnp.float32)
    sig = jax.nn.sigmoid(gate)
    act = gate * sig
    hidden = (act * up).astype(jnp.bfloat16)
    hid_split = hidden.astype(jnp.float32).reshape(count, N_DP, fpart)
    parts = jnp.einsum("rpf,pfd->prd", hid_split, wd.astype(jnp.float32).reshape(N_DP, fpart, D))
    expert_out = round_groups(parts)
    dact = jnp.dot(dy_rows, wd.T, preferred_element_type=jnp.float32)
    grad_hg = (dact * up * sig * (1.0 + gate * (1.0 - sig))).astype(jnp.bfloat16)
    grad_hu = (dact * act).astype(jnp.bfloat16)
    grad_wd = jnp.dot(hidden.T, dy_rows, preferred_element_type=jnp.float32).astype(jnp.bfloat16)
    grad_wg = jnp.dot(x_rows.T, grad_hg, preferred_element_type=jnp.float32).astype(jnp.bfloat16)
    grad_wu = jnp.dot(x_rows.T, grad_hu, preferred_element_type=jnp.float32).astype(jnp.bfloat16)
    back_parts = jnp.einsum("rpf,dpf->prd", grad_hg.astype(jnp.float32).reshape(count, N_DP, fpart),
                            wg.astype(jnp.float32).reshape(D, N_DP, fpart))
    back_parts = back_parts + jnp.einsum("rpf,dpf->prd", grad_hu.astype(jnp.float32).reshape(count, N_DP, fpart),
                                         wu.astype(jnp.float32).reshape(D, N_DP, fpart))
    token_part = round_groups(back_parts)
    return expert_out, token_part, grad_wg, grad_wu, grad_wd


def reference(tokens, expert_ids, gate_weights, w_gate, w_up, w_down, cotangent):
    blocks = TOKENS // TOK_DEV
    flat = expert_ids.reshape(blocks, TOK_DEV * TOP)
    onehot = (flat[:, :, None] == jnp.arange(EXPERTS, dtype=jnp.int32)[None, None, :]).astype(jnp.int32)
    before = jnp.sum((jnp.cumsum(onehot, axis=1) - onehot) * onehot, axis=2)
    column = jnp.arange(blocks, dtype=jnp.int32)[:, None] * CAP + before
    eflat = flat.reshape(-1).astype(jnp.int32)
    cflat = column.reshape(-1).astype(jnp.int32)
    rows_x = jnp.repeat(tokens, TOP, axis=0)
    buf_x = jnp.zeros((EXPERTS, blocks * CAP, D), jnp.bfloat16).at[eflat, cflat].set(rows_x)
    rows_d = (gate_weights[:, :, None] * cotangent[:, None, :].astype(jnp.float32)).reshape(TOKENS * TOP, D)
    buf_d = jnp.zeros((EXPERTS, blocks * CAP, D), jnp.bfloat16).at[eflat, cflat].set(rows_d.astype(jnp.bfloat16))
    expert_out, token_part, grad_gate, grad_up, grad_down = lax.map(expert_pass, (buf_x, buf_d, w_gate, w_up, w_down))
    picked = expert_out[eflat, cflat].astype(jnp.float32).reshape(TOKENS, TOP, D)
    mixed = jnp.sum(gate_weights[:, :, None] * picked, axis=1).astype(jnp.bfloat16)
    back = token_part[eflat, cflat].astype(jnp.float32).reshape(TOKENS, TOP, D)
    grad_tokens = jnp.sum(back, axis=1).astype(jnp.bfloat16)
    return mixed, grad_tokens, grad_gate, grad_up, grad_down
```

```python
import functools

import jax
import jax.numpy as jnp
from jax import lax
from jax.experimental import pallas as pl
from jax.experimental.pallas import tpu as pltpu
from jax.sharding import PartitionSpec as P

BF = jnp.bfloat16
F32 = jnp.float32
NN = (((1,), (0,)), ((), ()))
NT = (((1,), (1,)), ((), ()))
TN = (((0,), (0,)), ((), ()))
VMEM_LIMIT = 56 * 1024 * 1024


def dot(a, b, dims=NN):
    return lax.dot_general(a, b, dims, preferred_element_type=F32)


def params():
    return pltpu.CompilerParams(vmem_limit_bytes=VMEM_LIMIT)


def whole(shape):
    return pl.BlockSpec(shape, lambda *_: (0,) * len(shape))


def places(ids, experts):
    toks, top = ids.shape
    lanes = lax.broadcasted_iota(jnp.int32, (toks, experts), 1)
    hot = [(ids[:, k : k + 1] == lanes).astype(F32) for k in range(top)]
    earlier = (
        lax.broadcasted_iota(jnp.int32, (toks, toks), 1)
        < lax.broadcasted_iota(jnp.int32, (toks, toks), 0)
    ).astype(BF)
    counts = dot(earlier, sum(hot).astype(BF))
    return [jnp.sum(counts * h, axis=1, keepdims=True).astype(jnp.int32) for h in hot]


def place_kernel(experts, local, cap, pos, ids_ref, gw_ref, tok_ref, cot_ref, *outs):
    ids = ids_ref[...]
    gw = gw_ref[...]
    toks, top = ids.shape
    owners = experts // local
    here = places(ids, experts)
    rel = jnp.bitwise_xor(ids // local, pos[1])
    lanes = lax.broadcasted_iota(jnp.int32, (toks, local * cap), 1)
    col = [(ids[:, k : k + 1] % local) * cap + here[k] for k in range(top)]
    cot = cot_ref[...].astype(F32)
    scaled = [(gw[:, k : k + 1] * cot).astype(BF) for k in range(top)]
    tok = tok_ref[...]
    for j in range(owners):
        sel = [
            jnp.where((rel[:, k : k + 1] == j) & (col[k] == lanes), 1.0, 0.0).astype(BF)
            for k in range(top)
        ]
        outs[j][...] = dot(sum(sel), tok, TN).astype(BF)
        outs[owners + j][...] = sum(dot(sel[k], scaled[k], TN) for k in range(top)).astype(BF)


def place(pos, ids, gw, tokens, cot, experts, local, cap):
    toks, width = tokens.shape
    owners = experts // local
    shape = (local * cap, width)
    return pl.pallas_call(
        functools.partial(place_kernel, experts, local, cap),
        grid_spec=pltpu.PrefetchScalarGridSpec(
            num_scalar_prefetch=1,
            grid=(1,),
            in_specs=[whole(a.shape) for a in (ids, gw, tokens, cot)],
            out_specs=[whole(shape)] * (2 * owners),
        ),
        out_shape=[jax.ShapeDtypeStruct(shape, BF)] * (2 * owners),
        compiler_params=params(),
        name="place",
    )(pos, ids, gw, tokens, cot)


def pack_kernel(owners, cap, pos, *refs):
    mine, theirs, out = refs[:owners], refs[owners : 2 * owners], refs[-1]
    size = mine[0].shape[0]
    row = lax.broadcasted_iota(jnp.int32, (size, size), 0)
    column = lax.broadcasted_iota(jnp.int32, (size, size), 1)
    first = pos[0] * cap
    keep = jnp.where((row < cap) & (column == first + row), 1.0, 0.0).astype(BF)
    take = jnp.where((row >= cap) & (column == first + row - cap), 1.0, 0.0).astype(BF)
    parts = [dot(keep, mine[j][...]) + dot(take, theirs[j][...]) for j in range(owners)]
    out[...] = jnp.concatenate(parts, axis=0).astype(BF)


def pack(pos, mine, theirs, cap):
    size, width = mine[0].shape
    owners = len(mine)
    shape = (owners * size, width)
    return pl.pallas_call(
        functools.partial(pack_kernel, owners, cap),
        grid_spec=pltpu.PrefetchScalarGridSpec(
            num_scalar_prefetch=1,
            grid=(1,),
            in_specs=[whole((size, width))] * (2 * owners),
            out_specs=whole(shape),
        ),
        out_shape=jax.ShapeDtypeStruct(shape, BF),
        compiler_params=params(),
        name="pack",
    )(pos, *mine, *theirs)


def forward_kernel(chips, steps, pos, *refs):
    xs = refs[:chips]
    weights = refs[chips : chips + 6]
    ps = refs[chips + 6 : 2 * chips + 6]
    f1, f2, at, x, acc = refs[2 * chips + 6 :]
    step = pl.program_id(0)
    size = xs[0].shape[0]

    @pl.when(step == 0)
    def _():
        for i in range(chips):
            x[i * size : (i + 1) * size, :] = xs[i][...]

    rows = x[...]
    total = None
    for half in range(2):
        wg, wu, wd = weights[3 * half : 3 * half + 3]
        if half == 0:
            wg, wu, wd = wg.at[0], wu.at[0], wd.at[0]
        gate = dot(rows, wg[...])
        up = dot(rows, wu[...])
        sig = 1.0 / (1.0 + jnp.exp(-gate))
        act = gate * sig
        hidden = (act * up).astype(BF)
        f1[half] = (up * sig * (1.0 + gate * (1.0 - sig))).astype(BF)
        f2[half] = act.astype(BF)
        at[half] = hidden.T
        term = dot(hidden, wd[...])
        total = term if total is None else total + term

    @pl.when(step == 0)
    def _():
        acc[...] = total

    @pl.when(step > 0)
    def _():
        acc[...] += total

    @pl.when(step == steps - 1)
    def _():
        for i in range(chips):
            ps[i][...] = acc[i * size : (i + 1) * size, :].astype(BF)


def weight_specs(width, tile):
    return [
        pl.BlockSpec((1, width, tile), lambda f, pos: (pos[0], 0, f)),
        pl.BlockSpec((1, width, tile), lambda f, pos: (pos[0], 0, f)),
        pl.BlockSpec((1, tile, width), lambda f, pos: (pos[0], f, 0)),
        pl.BlockSpec((width, tile), lambda f, pos: (0, f)),
        pl.BlockSpec((width, tile), lambda f, pos: (0, f)),
        pl.BlockSpec((tile, width), lambda f, pos: (f, 0)),
    ]


def tile_of(hidden):
    return 256 if hidden % 256 == 0 else hidden


def forward(pos, xs, own, other):
    chips = len(xs)
    size, width = xs[0].shape
    hidden = other[0].shape[1]
    tile = tile_of(hidden)
    steps = hidden // tile
    rows = chips * size
    factor = pl.BlockSpec((2, rows, tile), lambda f, pos: (0, 0, f))
    out = pl.pallas_call(
        functools.partial(forward_kernel, chips, steps),
        grid_spec=pltpu.PrefetchScalarGridSpec(
            num_scalar_prefetch=1,
            grid=(steps,),
            in_specs=[whole((size, width))] * chips + weight_specs(width, tile),
            out_specs=[whole((size, width))] * chips
            + [factor, factor, pl.BlockSpec((2, tile, rows), lambda f, pos: (0, f, 0))],
            scratch_shapes=[pltpu.VMEM((rows, width), BF), pltpu.VMEM((rows, width), F32)],
        ),
        out_shape=[jax.ShapeDtypeStruct((size, width), BF)] * chips
        + [
            jax.ShapeDtypeStruct((2, rows, hidden), BF),
            jax.ShapeDtypeStruct((2, rows, hidden), BF),
            jax.ShapeDtypeStruct((2, hidden, rows), BF),
        ],
        cost_estimate=pl.CostEstimate(
            flops=12 * rows * width * hidden, bytes_accessed=12 * width * hidden, transcendentals=0
        ),
        compiler_params=params(),
        name="forward",
    )(pos, *xs, *own, *other)
    return out[:chips], out[chips], out[chips + 1], out[chips + 2]


def backward_kernel(chips, steps, pos, *refs):
    dys = refs[:chips]
    weights = refs[chips : chips + 6]
    f1, f2 = refs[chips + 6 : chips + 8]
    qs = refs[chips + 8 : 2 * chips + 8]
    dg, du, dy, acc = refs[2 * chips + 8 :]
    step = pl.program_id(0)
    size = dys[0].shape[0]

    @pl.when(step == 0)
    def _():
        for i in range(chips):
            dy[i * size : (i + 1) * size, :] = dys[i][...]

    rows = dy[...]
    total = None
    for half in range(2):
        wg, wu, wd = weights[3 * half : 3 * half + 3]
        if half == 0:
            wg, wu, wd = wg.at[0], wu.at[0], wd.at[0]
        da = dot(rows, wd[...], NT)
        grad_g = (da * f1[half].astype(F32)).astype(BF)
        grad_u = (da * f2[half].astype(F32)).astype(BF)
        dg[half] = grad_g
        du[half] = grad_u
        term = dot(grad_g, wg[...], NT) + dot(grad_u, wu[...], NT)
        total = term if total is None else total + term

    @pl.when(step == 0)
    def _():
        acc[...] = total

    @pl.when(step > 0)
    def _():
        acc[...] += total

    @pl.when(step == steps - 1)
    def _():
        for i in range(chips):
            qs[i][...] = acc[i * size : (i + 1) * size, :].astype(BF)


def backward(pos, dys, own, other, f1, f2):
    chips = len(dys)
    size, width = dys[0].shape
    hidden = other[0].shape[1]
    tile = tile_of(hidden)
    steps = hidden // tile
    rows = chips * size
    factor = pl.BlockSpec((2, rows, tile), lambda f, pos: (0, 0, f))
    out = pl.pallas_call(
        functools.partial(backward_kernel, chips, steps),
        grid_spec=pltpu.PrefetchScalarGridSpec(
            num_scalar_prefetch=1,
            grid=(steps,),
            in_specs=[whole((size, width))] * chips + weight_specs(width, tile) + [factor, factor],
            out_specs=[whole((size, width))] * chips + [factor, factor],
            scratch_shapes=[pltpu.VMEM((rows, width), BF), pltpu.VMEM((rows, width), F32)],
        ),
        out_shape=[jax.ShapeDtypeStruct((size, width), BF)] * chips
        + [jax.ShapeDtypeStruct((2, rows, hidden), BF)] * 2,
        cost_estimate=pl.CostEstimate(
            flops=12 * rows * width * hidden, bytes_accessed=12 * width * hidden, transcendentals=0
        ),
        compiler_params=params(),
        name="backward",
    )(pos, *dys, *own, *other, f1, f2)
    return out[:chips], out[chips], out[chips + 1]


def grads_kernel(chips, pos, *refs):
    xs = refs[:chips]
    dys = refs[chips : 2 * chips]
    dg, du, at = refs[2 * chips : 2 * chips + 3]
    own = refs[2 * chips + 3 : 2 * chips + 6]
    other = refs[2 * chips + 6 : 2 * chips + 9]
    xt, dy = refs[2 * chips + 9 :]
    size = xs[0].shape[0]

    @pl.when(pl.program_id(0) == 0)
    def _():
        for i in range(chips):
            dy[i * size : (i + 1) * size, :] = dys[i][...]
        xt[...] = jnp.concatenate([xs[i][...] for i in range(chips)], axis=0).T

    for half in range(2):
        gg = dot(xt[...], dg[half]).astype(BF)
        gu = dot(xt[...], du[half]).astype(BF)
        gd = dot(at[half], dy[...]).astype(BF)
        if half == 0:
            own[0][0], own[1][0], own[2][0] = gg, gu, gd
        else:
            other[0][...], other[1][...], other[2][...] = gg, gu, gd


def grads(pos, xs, dys, dg, du, at, local):
    chips = len(xs)
    size, width = xs[0].shape
    rows = chips * size
    hidden = dg.shape[2]
    tile = tile_of(hidden)
    steps = hidden // tile
    factor = pl.BlockSpec((2, rows, tile), lambda f, pos: (0, 0, f))
    wide = jax.ShapeDtypeStruct((local, width, hidden), BF)
    tall = jax.ShapeDtypeStruct((local, hidden, width), BF)
    out = pl.pallas_call(
        functools.partial(grads_kernel, chips),
        grid_spec=pltpu.PrefetchScalarGridSpec(
            num_scalar_prefetch=1,
            grid=(steps,),
            in_specs=[whole((size, width))] * (2 * chips)
            + [factor, factor, pl.BlockSpec((2, tile, rows), lambda f, pos: (0, f, 0))],
            out_specs=weight_specs(width, tile),
            scratch_shapes=[pltpu.VMEM((width, rows), BF), pltpu.VMEM((rows, width), BF)],
        ),
        out_shape=[
            wide,
            wide,
            tall,
            jax.ShapeDtypeStruct(wide.shape[1:], BF),
            jax.ShapeDtypeStruct(wide.shape[1:], BF),
            jax.ShapeDtypeStruct(tall.shape[1:], BF),
        ],
        cost_estimate=pl.CostEstimate(
            flops=12 * rows * width * hidden, bytes_accessed=12 * width * hidden, transcendentals=0
        ),
        compiler_params=params(),
        name="grads",
    )(pos, *xs, *dys, dg, du, at)
    return out[:3], out[3:]


def add_kernel(parts, *refs):
    total = refs[0][...].astype(F32)
    for ref in refs[1:parts]:
        total = total + ref[...].astype(F32)
    outs = refs[parts:]
    size = total.shape[0] // len(outs)
    for j, out in enumerate(outs):
        out[...] = total[j * size : (j + 1) * size].astype(BF)


def add(arrays, pieces=1):
    rows, width = arrays[0].shape
    shape = (rows // pieces, width)
    return pl.pallas_call(
        functools.partial(add_kernel, len(arrays)),
        grid=(1,),
        in_specs=[whole((rows, width))] * len(arrays),
        out_specs=[whole(shape)] * pieces,
        out_shape=[jax.ShapeDtypeStruct(shape, BF)] * pieces,
        compiler_params=params(),
        name="add",
    )(*arrays)


def combine_kernel(experts, local, cap, weighted, pos, ids_ref, gw_ref, *refs):
    owners = experts // local
    mine, theirs, out = refs[:owners], refs[owners : 2 * owners], refs[-1]
    ids = ids_ref[...]
    gw = gw_ref[...]
    toks, top = ids.shape
    here = places(ids, experts)
    size = mine[0].shape[0]
    lanes = lax.broadcasted_iota(jnp.int32, (toks, size), 1)
    total = jnp.zeros(out.shape, F32)
    for j in range(owners):
        for source, which in ((mine, 0), (theirs, 1)):
            expert = jnp.bitwise_xor(pos[1], j) * local + jnp.bitwise_xor(pos[0], which)
            mask = [
                (ids[:, k : k + 1] == expert) & (here[k] + which * cap == lanes) for k in range(top)
            ]
            values = source[j][...]
            if weighted:
                w = sum(jnp.where(mask[k], gw[:, k : k + 1], 0.0) for k in range(top))
                high = w.astype(BF)
                low = (w - high.astype(F32)).astype(BF)
                total = total + dot(high, values) + dot(low, values)
            else:
                w = sum(jnp.where(mask[k], 1.0, 0.0) for k in range(top))
                total = total + dot(w.astype(BF), values)
    out[...] = total.astype(BF)


def combine(pos, ids, gw, mine, theirs, experts, local, cap, weighted):
    size, width = mine[0].shape
    out = jax.ShapeDtypeStruct((ids.shape[0], width), BF)
    return pl.pallas_call(
        functools.partial(combine_kernel, experts, local, cap, weighted),
        grid_spec=pltpu.PrefetchScalarGridSpec(
            num_scalar_prefetch=1,
            grid=(1,),
            in_specs=[whole(ids.shape), whole(gw.shape)] + [whole((size, width))] * (2 * len(mine)),
            out_specs=whole(out.shape),
        ),
        out_shape=out,
        compiler_params=params(),
        name="combine",
    )(pos, ids, gw, *mine, *theirs)


def body(tokens, expert_ids, gate_weights, w_gate, w_up, w_down, cotangent):
    owners = lax.axis_size("expert")
    devices = lax.axis_size("dp")
    toks, width = tokens.shape
    top = expert_ids.shape[1]
    local = w_gate.shape[0]
    experts = local * owners
    cap = max(2, 5 * toks * top // (4 * experts))
    bits = (devices // 2).bit_length() - 1
    assert local == 2 and devices == 2 << bits and owners & (owners - 1) == 0

    core = lax.axis_index("dp") % 2
    pos = jnp.stack([core, lax.axis_index("expert")]).astype(jnp.int32)

    def to_pair(a):
        return lax.ppermute(a, "dp", [(i, i ^ 1) for i in range(devices)])

    def to_owner(a, j):
        return lax.ppermute(a, "expert", [(i, i ^ j) for i in range(owners)])

    def to_chip(a, s):
        def bit(i):
            return 2 << ((s + (i % 2) * (bits // 2)) % bits)

        return lax.ppermute(a, "dp", [(i, i ^ bit(i)) for i in range(devices)])

    def swap(messages):
        return [messages[0]] + [to_owner(messages[j], j) for j in range(1, owners)]

    def spread(messages):
        mine = swap(messages)
        theirs = [to_pair(m) for m in mine]
        parts = [pack(pos, mine, theirs, cap)]
        for s in range(bits):
            parts = parts + [to_chip(a, s) for a in parts]
        return parts

    def collect(parts):
        for s in reversed(range(1, bits)):
            half = len(parts) // 2
            arrived = [to_chip(a, s) for a in parts[half:]]
            sums = [parts[0]] + [add([parts[i], arrived[i]])[0] for i in range(1, half)]
            held = [arrived[0]] if s == bits - 1 else held + [arrived[0]]
            parts = sums
        held = [parts[0]] + (held if bits > 1 else []) + [to_chip(parts[1], 0)]
        mine = swap(add(held, owners))
        return mine, [to_pair(m) for m in mine]

    placed = place(pos, expert_ids, gate_weights, tokens, cotangent, experts, local, cap)
    own = (w_gate, w_up, w_down)
    other = [
        to_pair(lax.dynamic_index_in_dim(w, 1 - core, 0, keepdims=False)) for w in own
    ]
    xs = spread(placed[:owners])
    dys = spread(placed[owners:])
    ps, f1, f2, at = forward(pos, xs, own, other)
    qs, dg, du = backward(pos, dys, own, other, f1, f2)
    kept, given = grads(pos, xs, dys, dg, du, at, local)
    mine, theirs = collect(ps)
    mixed = combine(
        pos, expert_ids, gate_weights, mine, theirs, experts, local, cap, True
    )
    mine, theirs = collect(qs)
    grad_tokens = combine(
        pos, expert_ids, gate_weights, mine, theirs, experts, local, cap, False
    )
    got = [to_pair(g) for g in given]
    grad_gate, grad_up, grad_down = [
        lax.dynamic_update_index_in_dim(k, g, 1 - core, 0) for k, g in zip(kept, got)
    ]
    return (mixed, grad_tokens, grad_gate, grad_up, grad_down)


def solution(mesh):
    rows = P(("dp", "expert"), None)
    wide, tall = P("expert", None, "dp"), P("expert", "dp", None)
    return jax.shard_map(
        body,
        mesh=mesh,
        in_specs=(rows, rows, rows, wide, wide, tall, rows),
        out_specs=(rows, rows, wide, wide, tall),
        check_vma=False,
    )
```

```python
import functools

import jax
import jax.numpy as jnp
from jax import lax
from jax.experimental import pallas as pl
from jax.experimental.pallas import tpu as pltpu
from jax.sharding import PartitionSpec as P

BF = jnp.bfloat16
F32 = jnp.float32
NN = (((1,), (0,)), ((), ()))
NT = (((1,), (1,)), ((), ()))
TN = (((0,), (0,)), ((), ()))
MIB = 1024 * 1024
VMEM = pl.BlockSpec(memory_space=pltpu.VMEM)
SMEM = pl.BlockSpec(memory_space=pltpu.SMEM)
HBM = pl.BlockSpec(memory_space=pltpu.HBM)


def dot(a, b, dims=NN):
    return lax.dot_general(a, b, dims, preferred_element_type=F32)


def shaped(*shape):
    return jax.ShapeDtypeStruct(shape, BF)


def kernel_call(kernel, name, in_specs, out_specs, out_shape, scratch=(), limit=4, flops=0, alias=None):
    return pl.pallas_call(
        kernel,
        in_specs=in_specs,
        out_specs=out_specs,
        out_shape=out_shape,
        scratch_shapes=list(scratch),
        input_output_aliases=alias or {},
        cost_estimate=pl.CostEstimate(flops=flops, bytes_accessed=0, transcendentals=0),
        compiler_params=pltpu.CompilerParams(vmem_limit_bytes=limit * MIB),
        name=name,
    )


def places(ids, experts):
    top, toks = ids.shape
    rows = lax.broadcasted_iota(jnp.int32, (experts, toks), 0)
    hot = [(ids[k : k + 1, :] == rows).astype(F32) for k in range(top)]
    earlier = (
        lax.broadcasted_iota(jnp.int32, (toks, toks), 0)
        < lax.broadcasted_iota(jnp.int32, (toks, toks), 1)
    ).astype(BF)
    counts = dot(sum(hot).astype(BF), earlier)
    return [jnp.sum(counts * h, axis=0, keepdims=True).astype(jnp.int32) for h in hot]


def place_kernel(experts, local, cap, expert_pos, ids_hbm, gw_hbm, tok_hbm, cot_hbm, *refs):
    owners = experts // local
    outs = refs[: 2 * owners]
    ids_ref, gw_ref, tok_ref, cot_ref, sems = refs[2 * owners :]
    copies = [
        pltpu.make_async_copy(src, dst, sems.at[i])
        for i, (src, dst) in enumerate(
            ((ids_hbm, ids_ref), (gw_hbm, gw_ref), (tok_hbm, tok_ref), (cot_hbm, cot_ref))
        )
    ]
    for c in copies:
        c.start()
    copies[0].wait()
    copies[1].wait()
    ids = ids_ref[...]
    gw = gw_ref[...]
    top, toks = ids.shape
    here = places(ids, experts)
    rel = jnp.bitwise_xor(ids // local, expert_pos[0])
    rows = lax.broadcasted_iota(jnp.int32, (local * cap, toks), 0)
    col = [(ids[k : k + 1, :] % local) * cap + here[k] for k in range(top)]
    picks = []
    for j in range(owners):
        hits = [
            jnp.where((rel[k : k + 1, :] == j) & (col[k] == rows), 1.0, 0.0) for k in range(top)
        ]
        scale = jnp.sum(
            sum(hits[k] * gw[k : k + 1, :] for k in range(top)), axis=1, keepdims=True
        )
        picks.append((sum(hits).astype(BF), scale))
    copies[2].wait()
    for j in range(owners):
        outs[j][...] = dot(picks[j][0], tok_ref[...]).astype(BF)
    copies[3].wait()
    for j in range(owners):
        outs[owners + j][...] = (picks[j][1] * dot(picks[j][0], cot_ref[...])).astype(BF)


def place(expert_pos, ids, gw, tokens, cot, experts, local, cap):
    width = tokens.shape[1]
    owners = experts // local
    return kernel_call(
        functools.partial(place_kernel, experts, local, cap),
        "place",
        [SMEM] + [HBM] * 4,
        [VMEM] * (2 * owners),
        [shaped(local * cap, width)] * (2 * owners),
        [pltpu.VMEM(a.shape, a.dtype) for a in (ids, gw, tokens, cot)]
        + [pltpu.SemaphoreType.DMA((4,))],
    )(expert_pos, ids, gw, tokens, cot)


def pack_kernel(owners, cap, core, *refs):
    mine, theirs, out = refs[:owners], refs[owners : 2 * owners], refs[-1]
    size = mine[0].shape[0]
    row = lax.broadcasted_iota(jnp.int32, (size, size), 0)
    column = lax.broadcasted_iota(jnp.int32, (size, size), 1)
    first = core[0] * cap
    keep = jnp.where((row < cap) & (column == first + row), 1.0, 0.0).astype(BF)
    take = jnp.where((row >= cap) & (column == first + row - cap), 1.0, 0.0).astype(BF)
    parts = [dot(keep, mine[j][...]) + dot(take, theirs[j][...]) for j in range(owners)]
    out[...] = jnp.concatenate(parts, axis=0).astype(BF)


def pack(core, mine, theirs, cap):
    size, width = mine[0].shape
    owners = len(mine)
    return kernel_call(
        functools.partial(pack_kernel, owners, cap),
        "pack",
        [SMEM] + [VMEM] * (2 * owners),
        VMEM,
        shaped(owners * size, width),
    )(core, *mine, *theirs)


def fetch(core, weights, held, sems):
    return [
        pltpu.make_async_copy(w.at[core[0]], h, sems.at[i])
        for i, (w, h) in enumerate(zip(weights, held))
    ]


def gather_rows(parts, out):
    size = parts[0].shape[0]
    for i, part in enumerate(parts):
        out[i * size : (i + 1) * size, :] = part[...]


def tile_of(hidden):
    return 256 if hidden % 256 == 0 else hidden


def chunks(total, size):
    return [slice(i, min(i + size, total)) for i in range(0, total, size)]


def forward_kernel(chips, core, *refs):
    xs, own, other = refs[:chips], refs[chips : chips + 3], refs[chips + 3 : chips + 6]
    ps = refs[chips + 6 : 2 * chips + 6]
    x, f1, f2, hid, wg, wu, wd, gate_s, up_s, sems = refs[2 * chips + 6 :]
    loads = fetch(core, own, (wg, wu, wd), sems)
    for c in loads:
        c.start()
    gather_rows(xs, x)
    hidden = wg.shape[1]
    rows, width = x.shape
    size = rows // chips
    turn = 0
    for half, (a, b) in ((1, other[:2]), (0, (wg, wu))):
        if half == 0:
            loads[0].wait()
            loads[1].wait()
        for cols in chunks(hidden, tile_of(hidden)):
            gate_s[turn] = dot(x[...], a[:, cols])
            up_s[turn] = dot(x[...], b[:, cols])
            for r in chunks(rows, 64):
                gate, up = gate_s[turn, r], up_s[turn, r]
                sig = 1.0 / (1.0 + jnp.exp(-gate))
                act = gate * sig
                hid[half, r, cols] = (act * up).astype(BF)
                f1[half, r, cols] = (up * sig * (1.0 + gate * (1.0 - sig))).astype(BF)
                f2[half, r, cols] = act.astype(BF)
            turn = 1 - turn
    loads[2].wait()
    for cols in chunks(width, tile_of(width)):
        total = dot(hid[1], other[2][:, cols]) + dot(hid[0], wd[:, cols])
        for i in range(chips):
            ps[i][:, cols] = total[i * size : (i + 1) * size].astype(BF)


def forward(core, xs, own, other):
    chips = len(xs)
    size, width = xs[0].shape
    hidden = other[0].shape[1]
    rows = chips * size
    factor = shaped(2, rows, hidden)
    out = kernel_call(
        functools.partial(forward_kernel, chips),
        "forward",
        [SMEM] + [VMEM] * chips + [HBM] * 3 + [VMEM] * 3,
        [VMEM] * (chips + 4),
        [shaped(size, width)] * chips + [shaped(rows, width)] + [factor] * 3,
        [pltpu.VMEM(w.shape, BF) for w in other]
        + [pltpu.VMEM((2, rows, tile_of(hidden)), F32)] * 2
        + [pltpu.SemaphoreType.DMA((3,))],
        limit=32,
        flops=12 * rows * width * hidden,
    )(core, *xs, *own, *other)
    return out[:chips], *out[chips:]


def backward_kernel(chips, core, *refs):
    dys, own, other = refs[:chips], refs[chips : chips + 3], refs[chips + 3 : chips + 6]
    f1, f2 = refs[chips + 6 : chips + 8]
    qs = refs[chips + 8 : 2 * chips + 8]
    dy, dg, du, wg, wu, wd, da_s, sems = refs[2 * chips + 8 :]
    loads = fetch(core, own, (wg, wu, wd), sems)
    for i in (2, 0, 1):
        loads[i].start()
    gather_rows(dys, dy)
    hidden = wg.shape[1]
    rows, width = dy.shape
    size = rows // chips
    turn = 0
    for half, a in ((1, other[2]), (0, wd)):
        if half == 0:
            loads[2].wait()
        for cols in chunks(hidden, tile_of(hidden)):
            da_s[turn] = dot(dy[...], a[cols, :], NT)
            for r in chunks(rows, 64):
                da = da_s[turn, r]
                dg[half, r, cols] = (da * f1[half, r, cols].astype(F32)).astype(BF)
                du[half, r, cols] = (da * f2[half, r, cols].astype(F32)).astype(BF)
            turn = 1 - turn
    loads[0].wait()
    loads[1].wait()
    for cols in chunks(width, tile_of(width)):
        total = dot(dg[1], other[0][cols, :], NT) + dot(du[1], other[1][cols, :], NT)
        total = total + dot(dg[0], wg[cols, :], NT) + dot(du[0], wu[cols, :], NT)
        for i in range(chips):
            qs[i][:, cols] = total[i * size : (i + 1) * size].astype(BF)


def backward(core, dys, own, other, f1, f2):
    chips = len(dys)
    size, width = dys[0].shape
    hidden = other[0].shape[1]
    rows = chips * size
    factor = shaped(2, rows, hidden)
    out = kernel_call(
        functools.partial(backward_kernel, chips),
        "backward",
        [SMEM] + [VMEM] * chips + [HBM] * 3 + [VMEM] * 5,
        [VMEM] * (chips + 3),
        [shaped(size, width)] * chips + [shaped(rows, width)] + [factor] * 2,
        [pltpu.VMEM(w.shape, BF) for w in other]
        + [pltpu.VMEM((2, rows, tile_of(hidden)), F32)]
        + [pltpu.SemaphoreType.DMA((3,))],
        limit=32,
        flops=12 * rows * width * hidden,
    )(core, *dys, *own, *other, f1, f2)
    return out[:chips], *out[chips:]


def grads_kernel(core, x, dy, dg, du, hid, *refs):
    given, kept, held, sems = refs[:3], refs[3:6], refs[6:9], refs[9]
    hidden = dg.shape[2]
    width = x.shape[1]
    for half, outs in ((1, given), (0, held)):
        for cols in chunks(hidden, tile_of(hidden)):
            outs[0][:, cols] = dot(x[...], dg[half, :, cols], TN).astype(BF)
        if half == 0:
            save = [
                pltpu.make_async_copy(h, k.at[core[0]], sems.at[i])
                for i, (h, k) in enumerate(zip(held, kept))
            ]
            save[0].start()
        for cols in chunks(hidden, tile_of(hidden)):
            outs[1][:, cols] = dot(x[...], du[half, :, cols], TN).astype(BF)
        if half == 0:
            save[1].start()
        for cols in chunks(width, tile_of(width)):
            outs[2][:, cols] = dot(hid[half], dy[:, cols], TN).astype(BF)
        if half == 0:
            save[2].start()
            for c in save:
                c.wait()


def grads(core, x, dy, dg, du, hid, local):
    rows, width = x.shape
    hidden = dg.shape[2]
    shapes = [(width, hidden), (width, hidden), (hidden, width)]
    out = kernel_call(
        grads_kernel,
        "grads",
        [SMEM] + [VMEM] * 5,
        [VMEM] * 3 + [HBM] * 3,
        [shaped(*s) for s in shapes] + [shaped(local, *s) for s in shapes],
        [pltpu.VMEM(s, BF) for s in shapes] + [pltpu.SemaphoreType.DMA((3,))],
        limit=32,
        flops=12 * rows * width * hidden,
    )(core, x, dy, dg, du, hid)
    return out[:3], out[3:]


def finish_kernel(core, *refs):
    got, outs, sems = refs[:3], refs[6:9], refs[9]
    copies = [
        pltpu.make_async_copy(g, o.at[1 - core[0]], sems.at[i])
        for i, (g, o) in enumerate(zip(got, outs))
    ]
    for c in copies:
        c.start()
    for c in copies:
        c.wait()


def finish(core, got, kept):
    return kernel_call(
        finish_kernel,
        "finish",
        [SMEM] + [VMEM] * 3 + [HBM] * 3,
        [HBM] * 3,
        [shaped(*k.shape) for k in kept],
        [pltpu.SemaphoreType.DMA((3,))],
        limit=8,
        alias={4: 0, 5: 1, 6: 2},
    )(core, *got, *kept)


def add_kernel(parts, *refs):
    total = refs[0][...].astype(F32)
    for ref in refs[1:parts]:
        total = total + ref[...].astype(F32)
    outs = refs[parts:]
    size = total.shape[0] // len(outs)
    for j, out in enumerate(outs):
        out[...] = total[j * size : (j + 1) * size].astype(BF)


def add(arrays, pieces=1):
    rows, width = arrays[0].shape
    return kernel_call(
        functools.partial(add_kernel, len(arrays)),
        "add",
        [VMEM] * len(arrays),
        [VMEM] * pieces,
        [shaped(rows // pieces, width)] * pieces,
    )(*arrays)


def combine_kernel(experts, local, cap, weighted, core, expert_pos, ids_ref, gw_ref, *refs):
    owners = experts // local
    mine, theirs, out = refs[:owners], refs[owners : 2 * owners], refs[-1]
    ids = ids_ref[...]
    gw = gw_ref[...]
    top, toks = ids.shape
    here = places(ids, experts)
    size = mine[0].shape[0]
    rows = lax.broadcasted_iota(jnp.int32, (size, toks), 0)
    total = jnp.zeros(out.shape, F32)
    for j in range(owners):
        for source, which in ((mine, 0), (theirs, 1)):
            expert = jnp.bitwise_xor(expert_pos[0], j) * local + jnp.bitwise_xor(core[0], which)
            mask = [
                (ids[k : k + 1, :] == expert) & (here[k] + which * cap == rows) for k in range(top)
            ]
            values = source[j][...]
            if weighted:
                w = sum(jnp.where(mask[k], gw[k : k + 1, :], 0.0) for k in range(top))
                high = w.astype(BF)
                low = (w - high.astype(F32)).astype(BF)
                total = total + dot(high, values, TN) + dot(low, values, TN)
            else:
                w = sum(jnp.where(mask[k], 1.0, 0.0) for k in range(top))
                total = total + dot(w.astype(BF), values, TN)
    out[...] = total.astype(BF)


def combine(core, expert_pos, ids, gw, mine, theirs, experts, local, cap, weighted):
    width = mine[0].shape[1]
    return kernel_call(
        functools.partial(combine_kernel, experts, local, cap, weighted),
        "combine",
        [SMEM, SMEM] + [VMEM] * (2 + 2 * len(mine)),
        VMEM,
        shaped(ids.shape[1], width),
    )(core, expert_pos, ids, gw, *mine, *theirs)


def body(tokens, expert_ids, gate_weights, w_gate, w_up, w_down, cotangent):
    owners = lax.axis_size("expert")
    devices = lax.axis_size("dp")
    toks, width = tokens.shape
    top = expert_ids.shape[1]
    local = w_gate.shape[0]
    experts = local * owners
    cap = max(2, 5 * toks * top // (4 * experts))
    bits = (devices // 2).bit_length() - 1
    assert local == 2 and devices == 2 << bits and owners & (owners - 1) == 0

    side = lax.axis_index("dp") % 2
    core = side.astype(jnp.int32).reshape(1)
    expert_pos = lax.axis_index("expert").astype(jnp.int32).reshape(1)
    ids, gw = expert_ids.T, gate_weights.T

    def to_pair(a):
        return lax.ppermute(a, "dp", [(i, i ^ 1) for i in range(devices)])

    def to_owner(a, j):
        return lax.ppermute(a, "expert", [(i, i ^ j) for i in range(owners)])

    def to_chip(a, s):
        def bit(i):
            return 2 << ((s + (i % 2) * (bits // 2)) % bits)

        return lax.ppermute(a, "dp", [(i, i ^ bit(i)) for i in range(devices)])

    def swap(messages):
        return [messages[0]] + [to_owner(messages[j], j) for j in range(1, owners)]

    def spread(messages):
        mine = swap(messages)
        theirs = [to_pair(m) for m in mine]
        parts = [pack(core, mine, theirs, cap)]
        for s in range(bits):
            parts = parts + [to_chip(a, s) for a in parts]
        return parts

    def collect(parts):
        held = []
        for s in reversed(range(1, bits)):
            half = len(parts) // 2
            arrived = [to_chip(a, s) for a in parts[half:]]
            held.append(arrived[0])
            parts = [parts[0]] + [add([parts[i], arrived[i]])[0] for i in range(1, half)]
        held = [parts[0]] + held + [to_chip(parts[1], 0)]
        mine = swap(add(held, owners))
        return mine, [to_pair(m) for m in mine]

    placed = place(expert_pos, ids, gw, tokens, cotangent, experts, local, cap)
    own = (w_gate, w_up, w_down)
    other = [to_pair(lax.dynamic_index_in_dim(w, 1 - side, 0, keepdims=False)) for w in own]
    xs = spread(placed[:owners])
    dys = spread(placed[owners:])
    ps, x, f1, f2, hid = forward(core, xs, own, other)
    qs, dy, dg, du = backward(core, dys, own, other, f1, f2)
    given, kept = grads(core, x, dy, dg, du, hid, local)
    mine, theirs = collect(ps)
    mixed = combine(core, expert_pos, ids, gw, mine, theirs, experts, local, cap, True)
    mine, theirs = collect(qs)
    grad_tokens = combine(core, expert_pos, ids, gw, mine, theirs, experts, local, cap, False)
    grad_gate, grad_up, grad_down = finish(core, [to_pair(g) for g in given], kept)
    return (mixed, grad_tokens, grad_gate, grad_up, grad_down)


def solution(mesh):
    rows = P(("dp", "expert"), None)
    wide, tall = P("expert", None, "dp"), P("expert", "dp", None)
    return jax.shard_map(
        body,
        mesh=mesh,
        in_specs=(rows, rows, rows, wide, wide, tall, rows),
        out_specs=(rows, rows, wide, wide, tall),
        check_vma=False,
    )
```

```python
import functools

import jax
import jax.numpy as jnp
from jax import lax
from jax.experimental import pallas as pl
from jax.experimental.pallas import tpu as pltpu
from jax.sharding import PartitionSpec as P

BF = jnp.bfloat16
F32 = jnp.float32
NN = (((1,), (0,)), ((), ()))
NT = (((1,), (1,)), ((), ()))
TN = (((0,), (0,)), ((), ()))
MIB = 1024 * 1024
FLOPS_PER_US = 1153000000
VMEM = pl.BlockSpec(memory_space=pltpu.VMEM)
SMEM = pl.BlockSpec(memory_space=pltpu.SMEM)
HBM = pl.BlockSpec(memory_space=pltpu.HBM)
ANY = pl.BlockSpec(memory_space=pl.ANY)


def dot(a, b, dims=NN):
    return lax.dot_general(a, b, dims, preferred_element_type=F32)


def shaped(*shape):
    return jax.ShapeDtypeStruct(shape, BF)


def kernel_call(
    kernel, name, in_specs, out_specs, out_shape, scratch=(), limit=4, flops=0, alias=None, after=()
):
    count = len(in_specs)

    def run(*refs):
        kernel(*refs[:count], *refs[count + len(after) :])

    call = pl.pallas_call(
        run,
        in_specs=list(in_specs) + [ANY] * len(after),
        out_specs=out_specs,
        out_shape=out_shape,
        scratch_shapes=list(scratch),
        input_output_aliases=alias or {},
        cost_estimate=pl.CostEstimate(flops=flops, bytes_accessed=0, transcendentals=0),
        compiler_params=pltpu.CompilerParams(vmem_limit_bytes=limit * MIB),
        name=name,
    )
    return lambda *operands: call(*operands, *after)


def places(ids, experts):
    top, toks = ids.shape
    rows = lax.broadcasted_iota(jnp.int32, (experts, toks), 0)
    hot = [(ids[k : k + 1, :] == rows).astype(F32) for k in range(top)]
    earlier = (
        lax.broadcasted_iota(jnp.int32, (toks, toks), 0)
        < lax.broadcasted_iota(jnp.int32, (toks, toks), 1)
    ).astype(BF)
    counts = dot(sum(hot).astype(BF), earlier)
    return [jnp.sum(counts * h, axis=0, keepdims=True).astype(jnp.int32) for h in hot]


def start_all(pairs, sems):
    copies = [pltpu.make_async_copy(a, b, sems.at[i]) for i, (a, b) in enumerate(pairs)]
    for c in copies:
        c.start()
    return copies


def picks(ids, local, cap, experts, owner):
    top, toks = ids.shape
    here = places(ids, experts)
    rows = lax.broadcasted_iota(jnp.int32, (local * cap, toks), 0)
    return [
        jnp.where(
            (ids[k : k + 1, :] // local == owner)
            & ((ids[k : k + 1, :] % local) * cap + here[k] == rows),
            1.0,
            0.0,
        )
        for k in range(top)
    ]


def place_rows_kernel(experts, local, cap, expert_pos, ids_hbm, tok_hbm, out, chosen, *refs):
    ids_ref, tok_ref, sems = refs
    copies = start_all(((ids_hbm, ids_ref), (tok_hbm, tok_ref)), sems)
    copies[0].wait()
    ids = ids_ref[...]
    hits = []
    for j in range(experts // local):
        owner = jnp.bitwise_xor(expert_pos[0], j)
        hits.append(sum(picks(ids, local, cap, experts, owner)))
    chosen[...] = jnp.concatenate(hits, axis=0).astype(BF)
    copies[1].wait()
    out[...] = dot(chosen[...], tok_ref[...]).astype(BF)


def place_rows(expert_pos, ids, tokens, experts, local, cap):
    toks, width = tokens.shape
    return kernel_call(
        functools.partial(place_rows_kernel, experts, local, cap),
        "place_rows",
        [SMEM] + [HBM] * 2,
        [VMEM] * 2,
        [shaped(experts * cap, width), shaped(experts * cap, toks)],
        [pltpu.VMEM(a.shape, a.dtype) for a in (ids, tokens)] + [pltpu.SemaphoreType.DMA((2,))],
    )(expert_pos, ids, tokens)


def place_scaled_kernel(experts, local, cap, expert_pos, ids_hbm, gw_hbm, cot_hbm, *refs):
    out, high, low, ids_ref, gw_ref, cot_ref, sems = refs
    copies = start_all(((ids_hbm, ids_ref), (gw_hbm, gw_ref), (cot_hbm, cot_ref)), sems)
    copies[0].wait()
    copies[1].wait()
    ids = ids_ref[...]
    gw = gw_ref[...]
    hits, scales = [], []
    for j in range(experts // local):
        owner = jnp.bitwise_xor(expert_pos[0], j)
        hit = picks(ids, local, cap, experts, owner)
        hits.append(sum(hit))
        scales.append(sum(h * gw[k : k + 1, :] for k, h in enumerate(hit)))
    chosen = jnp.concatenate(hits, axis=0).astype(BF)
    scale = jnp.concatenate(scales, axis=0)
    high[...] = scale.astype(BF)
    low[...] = (scale - scale.astype(BF).astype(F32)).astype(BF)
    copies[2].wait()
    rows = dot(chosen, cot_ref[...])
    out[...] = (jnp.sum(scale, axis=1, keepdims=True) * rows).astype(BF)


def place_scaled(expert_pos, ids, gw, cot, experts, local, cap, after):
    toks, width = cot.shape
    return kernel_call(
        functools.partial(place_scaled_kernel, experts, local, cap),
        "place_scaled",
        [SMEM] + [HBM] * 3,
        [VMEM] * 3,
        [shaped(experts * cap, width)] + [shaped(experts * cap, toks)] * 2,
        [pltpu.VMEM(a.shape, a.dtype) for a in (ids, gw, cot)] + [pltpu.SemaphoreType.DMA((3,))],
        after=after,
    )(expert_pos, ids, gw, cot)


def blend_kernel(owners, cap, core, mine, theirs, *outs):
    size = mine.shape[0]
    part = size // owners
    row = lax.broadcasted_iota(jnp.int32, (size, size), 0)
    column = lax.broadcasted_iota(jnp.int32, (size, size), 1)
    first = core[0] * cap
    inside = row % part
    here = (inside >= first) & (inside < first + cap)
    shift = (1 - 2 * core[0]) * cap
    keep = jnp.where(here & (column == row), 1.0, 0.0).astype(BF)
    take = jnp.where((~here) & (column == row - shift), 1.0, 0.0).astype(BF)
    total = dot(keep, mine[...]) + dot(take, theirs[...])
    for j, out in enumerate(outs):
        out[...] = total[j * part : (j + 1) * part].astype(BF)


def blend(core, mine, theirs, owners, cap, after=()):
    size, width = mine.shape
    return kernel_call(
        functools.partial(blend_kernel, owners, cap),
        "blend",
        [SMEM] + [VMEM] * 2,
        [VMEM] * owners,
        [shaped(size // owners, width)] * owners,
        after=after,
    )(core, mine, theirs)


def join_kernel(*refs):
    parts, out = refs[:-1], refs[-1]
    out[...] = jnp.concatenate([p[...].astype(F32) for p in parts], axis=0).astype(BF)


def join(parts, after=(), flops=0):
    size, width = parts[0].shape
    return kernel_call(
        join_kernel,
        "join",
        [VMEM] * len(parts),
        VMEM,
        shaped(len(parts) * size, width),
        after=after,
        flops=flops,
    )(*parts)


def fetch(core, weights, held, sems):
    return start_all([(w.at[core[0]], h) for w, h in zip(weights, held)], sems)


def gather_rows(parts, out):
    first = 0
    for part in parts:
        out[first : first + part.shape[0], :] = part[...]
        first += part.shape[0]


def scatter_rows(total, parts, cols):
    first = 0
    for part in parts:
        part[:, cols] = total[first : first + part.shape[0]].astype(BF)
        first += part.shape[0]


def tile_of(hidden):
    return 256 if hidden % 256 == 0 else hidden


def chunks(total, size):
    return [slice(i, min(i + size, total)) for i in range(0, total, size)]


def forward_kernel(low, high, core, *refs):
    ps = refs[6:8]
    x, f1, f2, hid, g0, u0, d0, g1, u1, d1, gate_s, up_s, sems = refs[8:]
    own, other = refs[:3], refs[3:6]
    sources = (own[0], own[1], other[0], other[1], own[2], other[2])
    loads = fetch(core, sources, (g0, u0, g1, u1, d0, d1), sems)
    gather_rows((low, high), x)
    weights = ((g0, u0, d0), (g1, u1, d1))
    hidden = g0.shape[1]
    rows, width = x.shape
    turn = 0
    for half, (a, b, _) in enumerate(weights):
        loads[2 * half].wait()
        loads[2 * half + 1].wait()
        for cols in chunks(hidden, tile_of(hidden)):
            gate_s[turn] = dot(x[...], a[:, cols])
            up_s[turn] = dot(x[...], b[:, cols])
            for r in chunks(rows, 64):
                gate, up = gate_s[turn, r], up_s[turn, r]
                sig = 1.0 / (1.0 + jnp.exp(-gate))
                act = gate * sig
                hid[half, r, cols] = (act * up).astype(BF)
                f1[half, r, cols] = (up * sig * (1.0 + gate * (1.0 - sig))).astype(BF)
                f2[half, r, cols] = act.astype(BF)
            turn = 1 - turn
    loads[4].wait()
    loads[5].wait()
    for cols in chunks(width, tile_of(width)):
        total = dot(hid[0], d0[:, cols]) + dot(hid[1], d1[:, cols])
        scatter_rows(total, ps, cols)


def forward(core, xs, own, other):
    size, width = xs[0].shape
    hidden = own[0].shape[2]
    rows = 2 * size
    out = kernel_call(
        forward_kernel,
        "forward",
        [VMEM] * 2 + [SMEM] + [HBM] * 6,
        [VMEM] * 6,
        [shaped(size, width)] * 2 + [shaped(rows, width)] + [shaped(2, rows, hidden)] * 3,
        [pltpu.VMEM(w.shape[1:], BF) for w in own + own]
        + [pltpu.VMEM((2, rows, tile_of(hidden)), F32)] * 2
        + [pltpu.SemaphoreType.DMA((6,))],
        limit=32,
        flops=12 * rows * width * hidden,
    )(*xs, core, *own, *other)
    return out[:2], *out[2:]


def backward_kernel(low, high, core, *refs):
    f1, f2, qs = refs[6], refs[7], refs[8:10]
    dy, dg, du, g0, u0, d0, g1, u1, d1, da_s, sems = refs[10:]
    own, other = refs[:3], refs[3:6]
    sources = (own[2], other[2], own[0], own[1], other[0], other[1])
    loads = fetch(core, sources, (d0, d1, g0, u0, g1, u1), sems)
    gather_rows((low, high), dy)
    hidden = g0.shape[1]
    rows, width = dy.shape
    turn = 0
    for half, a in enumerate((d0, d1)):
        loads[half].wait()
        for cols in chunks(hidden, tile_of(hidden)):
            da_s[turn] = dot(dy[...], a[cols, :], NT)
            for r in chunks(rows, 64):
                da = da_s[turn, r]
                dg[half, r, cols] = (da * f1[half, r, cols].astype(F32)).astype(BF)
                du[half, r, cols] = (da * f2[half, r, cols].astype(F32)).astype(BF)
            turn = 1 - turn
    for c in loads[2:]:
        c.wait()
    for cols in chunks(width, tile_of(width)):
        total = dot(dg[0], g0[cols, :], NT) + dot(du[0], u0[cols, :], NT)
        total = total + dot(dg[1], g1[cols, :], NT) + dot(du[1], u1[cols, :], NT)
        scatter_rows(total, qs, cols)


def backward(core, dys, own, other, f1, f2):
    size, width = dys[0].shape
    hidden = own[0].shape[2]
    rows = 2 * size
    out = kernel_call(
        backward_kernel,
        "backward",
        [VMEM] * 2 + [SMEM] + [HBM] * 6 + [VMEM] * 2,
        [VMEM] * 5,
        [shaped(size, width)] * 2 + [shaped(rows, width)] + [shaped(2, rows, hidden)] * 2,
        [pltpu.VMEM(w.shape[1:], BF) for w in own + own]
        + [pltpu.VMEM((2, rows, tile_of(hidden)), F32)]
        + [pltpu.SemaphoreType.DMA((6,))],
        limit=32,
        flops=12 * rows * width * hidden,
    )(*dys, core, *own, *other, f1, f2)
    return out[:2], *out[2:]


def grads_kernel(half, core, x, dy, dg, du, hid, *refs):
    outs = [refs[0].at[i] for i in range(3)] if half else refs[3:6]
    hidden = dg.shape[2]
    width = x.shape[1]
    save = []

    def store(i):
        if not half:
            save.append(pltpu.make_async_copy(outs[i], refs[i].at[core[0]], refs[6].at[i]))
            save[i].start()

    for cols in chunks(hidden, tile_of(hidden)):
        outs[0][:, cols] = dot(x[...], dg[half, :, cols], TN).astype(BF)
    store(0)
    for cols in chunks(hidden, tile_of(hidden)):
        outs[1][:, cols] = dot(x[...], du[half, :, cols], TN).astype(BF)
    store(1)
    if half:
        for cols in chunks(hidden, tile_of(hidden)):
            outs[2][:, cols] = dot(dy[...], hid[half, :, cols], TN).astype(BF)
    else:
        for cols in chunks(width, tile_of(width)):
            outs[2][:, cols] = dot(hid[half], dy[:, cols], TN).astype(BF)
    store(2)
    for c in save:
        c.wait()


def grads(half, core, x, dy, dg, du, hid, local, after):
    rows, width = x.shape
    hidden = dg.shape[2]
    wide, tall = (width, hidden), (hidden, width)
    if half:
        outs, scratch = [shaped(3, *wide)], []
    else:
        outs = [shaped(local, *s) for s in (wide, wide, tall)]
        scratch = [pltpu.VMEM(s, BF) for s in (wide, wide, tall)] + [pltpu.SemaphoreType.DMA((3,))]
    return kernel_call(
        functools.partial(grads_kernel, half),
        "grads_given" if half else "grads_kept",
        [SMEM] + [VMEM] * 5,
        [VMEM if half else HBM] * len(outs),
        outs,
        scratch,
        limit=32,
        flops=6 * rows * width * hidden,
        after=after,
    )(core, x, dy, dg, du, hid)


def finish_kernel(core, got, *refs):
    outs, down, sems = refs[3:6], refs[6], refs[7]
    place = 1 - core[0]
    copies = start_all([(got.at[i], outs[i].at[place]) for i in range(2)], sems)
    down[...] = got[2].T
    copies += start_all([(down, outs[2].at[place])], sems.at[pl.ds(2, 1)])
    for c in copies:
        c.wait()


def finish(core, got, kept):
    return kernel_call(
        finish_kernel,
        "finish",
        [SMEM, VMEM] + [HBM] * 3,
        [HBM] * 3,
        [shaped(*k.shape) for k in kept],
        [pltpu.VMEM(kept[2].shape[1:], BF), pltpu.SemaphoreType.DMA((3,))],
        limit=14,
        alias={2: 0, 3: 1, 4: 2},
    )(core, got, *kept)


def add_kernel(first, second, *outs):
    total = first[...].astype(F32) + second[...].astype(F32)
    size = total.shape[0] // len(outs)
    for j, out in enumerate(outs):
        out[...] = total[j * size : (j + 1) * size].astype(BF)


def add(arrays, pieces=1, after=()):
    rows, width = arrays[0].shape
    return kernel_call(
        add_kernel,
        "add",
        [VMEM] * 2,
        [VMEM] * pieces,
        [shaped(rows // pieces, width)] * pieces,
        after=after,
    )(*arrays)


def combine_kernel(weights, *refs):
    messages, out = refs[weights:-1], refs[-1]
    values = jnp.concatenate([m[...].astype(F32) for m in messages], axis=0).astype(BF)
    out[...] = sum(dot(w[...], values, TN) for w in refs[:weights]).astype(BF)


def combine(weights, messages, after=()):
    return kernel_call(
        functools.partial(combine_kernel, len(weights)),
        "combine",
        [VMEM] * (len(weights) + len(messages)),
        VMEM,
        shaped(weights[0].shape[1], messages[0].shape[1]),
        after=after,
    )(*weights, *messages)


def body(tokens, expert_ids, gate_weights, w_gate, w_up, w_down, cotangent):
    owners = lax.axis_size("expert")
    devices = lax.axis_size("dp")
    toks, width = tokens.shape
    top = expert_ids.shape[1]
    local = w_gate.shape[0]
    experts = local * owners
    cap = max(2, 5 * toks * top // (4 * experts))
    bits = (devices // 2).bit_length() - 1
    assert local == 2 and devices == 2 << bits and owners & (owners - 1) == 0

    side = lax.axis_index("dp") % 2
    core = side.astype(jnp.int32).reshape(1)
    expert_pos = lax.axis_index("expert").astype(jnp.int32).reshape(1)
    ids, gw = expert_ids.T, gate_weights.T

    def to_pair(a):
        return lax.ppermute(a, "dp", [(i, i ^ 1) for i in range(devices)])

    def to_owner(a, j):
        return lax.ppermute(a, "expert", [(i, i ^ j) for i in range(owners)])

    def to_chip(a, s):
        def bit(i):
            return 2 << ((s + (i % 2) * (bits // 2)) % bits)

        return lax.ppermute(a, "dp", [(i, i ^ bit(i)) for i in range(devices)])

    def swap(messages):
        return [messages[0]] + [to_owner(messages[j], j) for j in range(1, owners)]

    def widen(part, after=()):
        for s in range(bits - 1):
            part = join([part, to_chip(part, s)], after)
        return part

    def reduce(low, high, after=()):
        for s in reversed(range(1, bits)):
            low, high = add([low, to_chip(high, s)], 2, after)
        return low, high

    def hand_out(rows, after=()):
        return blend(core, rows, to_pair(rows), owners, cap, after)

    own = (w_gate, w_up, w_down)
    rows, chosen = place_rows(expert_pos, ids, tokens, experts, local, cap)
    messages = hand_out(rows)
    rows, high, low = place_scaled(expert_pos, ids, gw, cotangent, experts, local, cap, [rows])
    scaled = hand_out(rows)
    joined = join(swap(messages), scaled[:1])
    joined_scaled = join(swap(scaled), [joined], 18 * FLOPS_PER_US)
    x_low = widen(joined)
    x_high = to_chip(x_low, bits - 1)
    *behind, _ = lax.optimization_barrier((*own, x_low))
    other = [to_pair(w) for w in behind]
    dy_low = widen(joined_scaled, [x_low])
    dy_high = to_chip(dy_low, bits - 1)
    ps, x, f1, f2, hid = forward(core, (x_low, x_high), own, other)
    qs, dy, dg, du = backward(core, (dy_low, dy_high), own, other, f1, f2)
    p_low, p_high = reduce(*ps, [dy])
    given = grads(1, core, x, dy, dg, du, hid, local, [p_high])
    q_low, q_high = reduce(*qs, given[:1])
    p_messages = hand_out(add([p_low, to_chip(p_high, 0)], 1, [q_high])[0])
    q_rows = add([q_low, to_chip(q_high, 0)], 1, p_messages[:1])[0]
    kept = grads(0, core, x, dy, dg, du, hid, local, [q_rows])
    p_messages = join(swap(p_messages), kept[:1], 20 * FLOPS_PER_US)
    q_messages = hand_out(q_rows, [p_messages])
    mixed = combine([high, low], [p_messages], q_messages[:1])
    behind, _ = lax.optimization_barrier((given[0], q_messages[0]))
    got = to_pair(behind)
    grad_gate, grad_up, grad_down = finish(core, got, kept)
    grad_tokens = combine([chosen], swap(q_messages), [grad_gate])
    return (mixed, grad_tokens, grad_gate, grad_up, grad_down)


def solution(mesh):
    rows = P(("dp", "expert"), None)
    wide, tall = P("expert", None, "dp"), P("expert", "dp", None)
    return jax.shard_map(
        body,
        mesh=mesh,
        in_specs=(rows, rows, rows, wide, wide, tall, rows),
        out_specs=(rows, rows, wide, wide, tall),
        check_vma=False,
    )
```

```python
import functools

import jax
import jax.numpy as jnp
from jax import lax
from jax.experimental import pallas as pl
from jax.experimental.pallas import tpu as pltpu
from jax.sharding import PartitionSpec as P

BF = jnp.bfloat16
F32 = jnp.float32
NN = (((1,), (0,)), ((), ()))
NT = (((1,), (1,)), ((), ()))
TN = (((0,), (0,)), ((), ()))
MIB = 1024 * 1024
FLOPS_PER_US = 1153000000
VMEM = pl.BlockSpec(memory_space=pltpu.VMEM)
SMEM = pl.BlockSpec(memory_space=pltpu.SMEM)
HBM = pl.BlockSpec(memory_space=pltpu.HBM)
ANY = pl.BlockSpec(memory_space=pl.ANY)


def dot(a, b, dims=NN):
    return lax.dot_general(a, b, dims, preferred_element_type=F32)


def shaped(*shape):
    return jax.ShapeDtypeStruct(shape, BF)


TOKEN = shaped(16, 128)


def kernel_call(
    kernel, name, in_specs, out_specs, out_shape, scratch=(), limit=4, flops=0, alias=None, after=()
):
    count = len(in_specs)

    def run(*refs):
        kernel(*refs[:count], *refs[count + len(after) :])

    call = pl.pallas_call(
        run,
        in_specs=list(in_specs) + [ANY] * len(after),
        out_specs=out_specs,
        out_shape=out_shape,
        scratch_shapes=list(scratch),
        input_output_aliases=alias or {},
        cost_estimate=pl.CostEstimate(flops=flops, bytes_accessed=0, transcendentals=0),
        compiler_params=pltpu.CompilerParams(vmem_limit_bytes=limit * MIB),
        name=name,
    )
    return lambda *operands: call(*operands, *after)


def places(ids, experts):
    top, toks = ids.shape
    rows = lax.broadcasted_iota(jnp.int32, (experts, toks), 0)
    hot = [(ids[k : k + 1, :] == rows).astype(F32) for k in range(top)]
    earlier = (
        lax.broadcasted_iota(jnp.int32, (toks, toks), 0)
        < lax.broadcasted_iota(jnp.int32, (toks, toks), 1)
    ).astype(BF)
    counts = dot(sum(hot).astype(BF), earlier)
    return [jnp.sum(counts * h, axis=0, keepdims=True).astype(jnp.int32) for h in hot]


def start_all(pairs, sems):
    copies = [pltpu.make_async_copy(a, b, sems.at[i]) for i, (a, b) in enumerate(pairs)]
    for c in copies:
        c.start()
    return copies


def picks(ids, local, cap, experts, owner):
    top, toks = ids.shape
    here = places(ids, experts)
    rows = lax.broadcasted_iota(jnp.int32, (local * cap, toks), 0)
    return [
        jnp.where(
            (ids[k : k + 1, :] // local == owner)
            & ((ids[k : k + 1, :] % local) * cap + here[k] == rows),
            1.0,
            0.0,
        )
        for k in range(top)
    ]


def place_rows_kernel(experts, local, cap, expert_pos, ids_hbm, tok_hbm, out, chosen, *refs):
    ids_ref, tok_ref, sems = refs
    copies = start_all(((ids_hbm, ids_ref), (tok_hbm, tok_ref)), sems)
    copies[0].wait()
    ids = ids_ref[...]
    hits = []
    for j in range(experts // local):
        owner = jnp.bitwise_xor(expert_pos[0], j)
        hits.append(sum(picks(ids, local, cap, experts, owner)))
    chosen[...] = jnp.concatenate(hits, axis=0).astype(BF)
    copies[1].wait()
    out[...] = dot(chosen[...], tok_ref[...]).astype(BF)


def place_rows(expert_pos, ids, tokens, experts, local, cap):
    toks, width = tokens.shape
    return kernel_call(
        functools.partial(place_rows_kernel, experts, local, cap),
        "place_rows",
        [SMEM] + [HBM] * 2,
        [VMEM] * 2,
        [shaped(experts * cap, width), shaped(experts * cap, toks)],
        [pltpu.VMEM(a.shape, a.dtype) for a in (ids, tokens)] + [pltpu.SemaphoreType.DMA((2,))],
    )(expert_pos, ids, tokens)


def place_scaled_kernel(experts, local, cap, expert_pos, ids_hbm, gw_hbm, cot_hbm, *refs):
    out, high, low, ids_ref, gw_ref, cot_ref, sems = refs
    copies = start_all(((ids_hbm, ids_ref), (gw_hbm, gw_ref), (cot_hbm, cot_ref)), sems)
    copies[0].wait()
    copies[1].wait()
    ids = ids_ref[...]
    gw = gw_ref[...]
    hits, scales = [], []
    for j in range(experts // local):
        owner = jnp.bitwise_xor(expert_pos[0], j)
        hit = picks(ids, local, cap, experts, owner)
        hits.append(sum(hit))
        scales.append(sum(h * gw[k : k + 1, :] for k, h in enumerate(hit)))
    chosen = jnp.concatenate(hits, axis=0).astype(BF)
    scale = jnp.concatenate(scales, axis=0)
    high[...] = scale.astype(BF)
    low[...] = (scale - scale.astype(BF).astype(F32)).astype(BF)
    copies[2].wait()
    rows = dot(chosen, cot_ref[...])
    out[...] = (jnp.sum(scale, axis=1, keepdims=True) * rows).astype(BF)


def place_scaled(expert_pos, ids, gw, cot, experts, local, cap, after):
    toks, width = cot.shape
    return kernel_call(
        functools.partial(place_scaled_kernel, experts, local, cap),
        "place_scaled",
        [SMEM] + [HBM] * 3,
        [VMEM] * 3,
        [shaped(experts * cap, width)] + [shaped(experts * cap, toks)] * 2,
        [pltpu.VMEM(a.shape, a.dtype) for a in (ids, gw, cot)] + [pltpu.SemaphoreType.DMA((3,))],
        after=after,
    )(expert_pos, ids, gw, cot)


def blend_kernel(owners, cap, core, mine, theirs, *outs):
    size = mine.shape[0]
    part = size // owners
    row = lax.broadcasted_iota(jnp.int32, (size, size), 0)
    column = lax.broadcasted_iota(jnp.int32, (size, size), 1)
    first = core[0] * cap
    inside = row % part
    here = (inside >= first) & (inside < first + cap)
    shift = (1 - 2 * core[0]) * cap
    keep = jnp.where(here & (column == row), 1.0, 0.0).astype(BF)
    take = jnp.where((~here) & (column == row - shift), 1.0, 0.0).astype(BF)
    total = dot(keep, mine[...]) + dot(take, theirs[...])
    for j, out in enumerate(outs):
        out[...] = total[j * part : (j + 1) * part].astype(BF)


def blend(core, mine, theirs, owners, cap, after=()):
    size, width = mine.shape
    return kernel_call(
        functools.partial(blend_kernel, owners, cap),
        "blend",
        [SMEM] + [VMEM] * 2,
        [VMEM] * owners,
        [shaped(size // owners, width)] * owners,
        after=after,
    )(core, mine, theirs)


def join_kernel(*refs):
    parts, out = refs[:-1], refs[-1]
    out[...] = jnp.concatenate([p[...].astype(F32) for p in parts], axis=0).astype(BF)


def join(parts, after=(), flops=0):
    size, width = parts[0].shape
    return kernel_call(
        join_kernel,
        "join",
        [VMEM] * len(parts),
        VMEM,
        shaped(len(parts) * size, width),
        after=after,
        flops=flops,
    )(*parts)


def gather_rows(parts, out):
    first = 0
    for part in parts:
        out[first : first + part.shape[0], :] = part[...]
        first += part.shape[0]


def scatter_rows(total, parts, cols):
    first = 0
    for part in parts:
        part[:, cols] = total[first : first + part.shape[0]].astype(BF)
        first += part.shape[0]


def tile_of(hidden):
    return 256 if hidden % 256 == 0 else hidden


def chunks(total, size):
    return [slice(i, min(i + size, total)) for i in range(0, total, size)]


def forward_kernel(low, high, core, *refs):
    ps = refs[6:8]
    x, f1, f2, hid, gate_s, up_s = refs[8:]
    g0, u0, d0, g1, u1, d1 = (w.at[core[0]] for w in refs[:6])
    gather_rows((low, high), x)
    weights = ((g0, u0, d0), (g1, u1, d1))
    hidden = g0.shape[1]
    rows, width = x.shape
    turn = 0
    for half, (a, b, _) in enumerate(weights):
        for cols in chunks(hidden, tile_of(hidden)):
            gate_s[turn] = dot(x[...], a[:, cols])
            up_s[turn] = dot(x[...], b[:, cols])
            for r in chunks(rows, 64):
                gate, up = gate_s[turn, r], up_s[turn, r]
                sig = 1.0 / (1.0 + jnp.exp(-gate))
                act = gate * sig
                hid[half, r, cols] = (act * up).astype(BF)
                f1[half, r, cols] = (up * sig * (1.0 + gate * (1.0 - sig))).astype(BF)
                f2[half, r, cols] = act.astype(BF)
            turn = 1 - turn
    for cols in chunks(width, tile_of(width)):
        total = dot(hid[0], d0[:, cols]) + dot(hid[1], d1[:, cols])
        scatter_rows(total, ps, cols)


def forward(core, xs, own, other):
    size, width = xs[0].shape
    hidden = own[0].shape[2]
    rows = 2 * size
    out = kernel_call(
        forward_kernel,
        "forward",
        [VMEM] * 2 + [SMEM] + [VMEM] * 6,
        [VMEM] * 6,
        [shaped(size, width)] * 2 + [shaped(rows, width)] + [shaped(2, rows, hidden)] * 3,
        [pltpu.VMEM((2, rows, tile_of(hidden)), F32)] * 2,
        limit=32,
        flops=12 * rows * width * hidden,
    )(*xs, core, *own, *other)
    return out[:2], *out[2:]


def backward_kernel(low, high, core, *refs):
    f1, f2, qs = refs[6], refs[7], refs[8:10]
    dy, dg, du, da_s = refs[10:]
    g0, u0, d0, g1, u1, d1 = (w.at[core[0]] for w in refs[:6])
    gather_rows((low, high), dy)
    hidden = g0.shape[1]
    rows, width = dy.shape
    turn = 0
    for half, a in enumerate((d0, d1)):
        for cols in chunks(hidden, tile_of(hidden)):
            da_s[turn] = dot(dy[...], a[cols, :], NT)
            for r in chunks(rows, 64):
                da = da_s[turn, r]
                dg[half, r, cols] = (da * f1[half, r, cols].astype(F32)).astype(BF)
                du[half, r, cols] = (da * f2[half, r, cols].astype(F32)).astype(BF)
            turn = 1 - turn
    for cols in chunks(width, tile_of(width)):
        total = dot(dg[0], g0[cols, :], NT) + dot(du[0], u0[cols, :], NT)
        total = total + dot(dg[1], g1[cols, :], NT) + dot(du[1], u1[cols, :], NT)
        scatter_rows(total, qs, cols)


def backward(core, dys, own, other, f1, f2):
    size, width = dys[0].shape
    hidden = own[0].shape[2]
    rows = 2 * size
    out = kernel_call(
        backward_kernel,
        "backward",
        [VMEM] * 2 + [SMEM] + [VMEM] * 8,
        [VMEM] * 5,
        [shaped(size, width)] * 2 + [shaped(rows, width)] + [shaped(2, rows, hidden)] * 2,
        [pltpu.VMEM((2, rows, tile_of(hidden)), F32)],
        limit=32,
        flops=12 * rows * width * hidden,
    )(*dys, core, *own, *other, f1, f2)
    return out[:2], *out[2:]


def grads_kernel(half, core, x, dy, dg, du, hid, *refs):
    *refs, token = refs if half else (*refs[:3], *refs[4:], refs[3])
    token[...] = jnp.zeros(token.shape, BF)
    outs = [refs[0].at[i] for i in range(3)] if half else refs[3:6]
    hidden = dg.shape[2]
    width = x.shape[1]
    save = []

    def store(i):
        if not half:
            save.append(pltpu.make_async_copy(outs[i], refs[i].at[core[0]], refs[6].at[i]))
            save[i].start()

    for cols in chunks(hidden, tile_of(hidden)):
        outs[0][:, cols] = dot(x[...], dg[half, :, cols], TN).astype(BF)
    store(0)
    for cols in chunks(hidden, tile_of(hidden)):
        outs[1][:, cols] = dot(x[...], du[half, :, cols], TN).astype(BF)
    store(1)
    if half:
        for cols in chunks(hidden, tile_of(hidden)):
            outs[2][:, cols] = dot(dy[...], hid[half, :, cols], TN).astype(BF)
    else:
        for cols in chunks(width, tile_of(width)):
            outs[2][:, cols] = dot(hid[half], dy[:, cols], TN).astype(BF)
    store(2)
    for c in save:
        c.wait()


def grads(half, core, x, dy, dg, du, hid, local, after):
    rows, width = x.shape
    hidden = dg.shape[2]
    wide, tall = (width, hidden), (hidden, width)
    if half:
        outs, scratch = [shaped(3, *wide)], []
    else:
        outs = [shaped(local, *s) for s in (wide, wide, tall)]
        scratch = [pltpu.VMEM(s, BF) for s in (wide, wide, tall)] + [pltpu.SemaphoreType.DMA((3,))]
    return kernel_call(
        functools.partial(grads_kernel, half),
        "grads_given" if half else "grads_kept",
        [SMEM] + [VMEM] * 5,
        [VMEM if half else HBM] * len(outs) + [VMEM],
        outs + [TOKEN],
        scratch,
        limit=32,
        flops=6 * rows * width * hidden,
        after=after,
    )(core, x, dy, dg, du, hid)


def finish_kernel(core, got, *refs):
    outs, token, down, sems = refs[3:6], refs[6], refs[7], refs[8]
    token[...] = jnp.zeros(token.shape, BF)
    place = 1 - core[0]
    copies = start_all([(got.at[i], outs[i].at[place]) for i in range(2)], sems)
    down[...] = got[2].T
    copies += start_all([(down, outs[2].at[place])], sems.at[pl.ds(2, 1)])
    for c in copies:
        c.wait()


def finish(core, got, kept, after):
    return kernel_call(
        finish_kernel,
        "finish",
        [SMEM, VMEM] + [HBM] * 3,
        [HBM] * 3 + [VMEM],
        [shaped(*k.shape) for k in kept] + [TOKEN],
        [pltpu.VMEM(kept[2].shape[1:], BF), pltpu.SemaphoreType.DMA((3,))],
        limit=14,
        alias={2: 0, 3: 1, 4: 2},
        after=after,
    )(core, got, *kept)


def add_kernel(first, second, *outs):
    total = first[...].astype(F32) + second[...].astype(F32)
    size = total.shape[0] // len(outs)
    for j, out in enumerate(outs):
        out[...] = total[j * size : (j + 1) * size].astype(BF)


def add(arrays, pieces=1, after=()):
    rows, width = arrays[0].shape
    return kernel_call(
        add_kernel,
        "add",
        [VMEM] * 2,
        [VMEM] * pieces,
        [shaped(rows // pieces, width)] * pieces,
        after=after,
    )(*arrays)


def combine_kernel(weights, *refs):
    messages, out = refs[weights:-1], refs[-1]
    values = jnp.concatenate([m[...].astype(F32) for m in messages], axis=0).astype(BF)
    out[...] = sum(dot(w[...], values, TN) for w in refs[:weights]).astype(BF)


def combine(weights, messages, after=()):
    return kernel_call(
        functools.partial(combine_kernel, len(weights)),
        "combine",
        [VMEM] * (len(weights) + len(messages)),
        VMEM,
        shaped(weights[0].shape[1], messages[0].shape[1]),
        after=after,
    )(*weights, *messages)


def body(tokens, expert_ids, gate_weights, w_gate, w_up, w_down, cotangent):
    owners = lax.axis_size("expert")
    devices = lax.axis_size("dp")
    toks, width = tokens.shape
    top = expert_ids.shape[1]
    local = w_gate.shape[0]
    experts = local * owners
    cap = max(2, 5 * toks * top // (4 * experts))
    bits = (devices // 2).bit_length() - 1
    assert local == 2 and devices == 2 << bits and owners & (owners - 1) == 0

    side = lax.axis_index("dp") % 2
    core = side.astype(jnp.int32).reshape(1)
    expert_pos = lax.axis_index("expert").astype(jnp.int32).reshape(1)
    ids, gw = expert_ids.T, gate_weights.T

    def to_pair(a):
        return lax.ppermute(a, "dp", [(i, i ^ 1) for i in range(devices)])

    def to_owner(a, j):
        return lax.ppermute(a, "expert", [(i, i ^ j) for i in range(owners)])

    def to_chip(a, s):
        def bit(i):
            return 2 << ((s + (i % 2) * (bits // 2)) % bits)

        return lax.ppermute(a, "dp", [(i, i ^ bit(i)) for i in range(devices)])

    def swap(messages):
        return [messages[0]] + [to_owner(messages[j], j) for j in range(1, owners)]

    def widen(part, after=()):
        for s in range(bits - 1):
            part = join([part, to_chip(part, s)], after)
        return part

    def reduce(low, high, after=()):
        for s in reversed(range(1, bits)):
            low, high = add([low, to_chip(high, s)], 2, after)
        return low, high

    def hand_out(rows, after=()):
        return blend(core, rows, to_pair(rows), owners, cap, after)

    own = (w_gate, w_up, w_down)
    rows, chosen = place_rows(expert_pos, ids, tokens, experts, local, cap)
    messages = hand_out(rows)
    rows, high, low = place_scaled(expert_pos, ids, gw, cotangent, experts, local, cap, [rows])
    scaled = hand_out(rows)
    joined = join(swap(messages), scaled[:1])
    joined_scaled = join(swap(scaled), [joined], 18 * FLOPS_PER_US)
    x_low = widen(joined)
    x_high = to_chip(x_low, bits - 1)
    *behind, _ = lax.optimization_barrier((*own, x_low))
    other = [to_pair(w) for w in behind]
    dy_low = widen(joined_scaled, [x_low])
    dy_high = to_chip(dy_low, bits - 1)
    ps, x, f1, f2, hid = forward(core, (x_low, x_high), own, other)
    qs, dy, dg, du = backward(core, (dy_low, dy_high), own, other, f1, f2)
    p_low, p_high = reduce(*ps, [dy])
    given, token = grads(1, core, x, dy, dg, du, hid, local, [p_high])
    *kept, token = grads(0, core, x, dy, dg, du, hid, local, [token])
    q_low, q_high = reduce(*qs, [token])
    p_messages = hand_out(add([p_low, to_chip(p_high, 0)], 1, [q_high])[0])
    q_rows = add([q_low, to_chip(q_high, 0)], 1, p_messages[:1])[0]
    p_messages = join(swap(p_messages), [q_rows], 20 * FLOPS_PER_US)
    q_messages = hand_out(q_rows, [p_messages])
    mixed = combine([high, low], [p_messages], q_messages[:1])
    behind, _ = lax.optimization_barrier((given, q_messages[0]))
    got = to_pair(behind)
    grad_gate, grad_up, grad_down, token = finish(core, got, kept, [mixed])
    grad_tokens = combine([chosen], swap(q_messages), [token])
    return (mixed, grad_tokens, grad_gate, grad_up, grad_down)


def solution(mesh):
    rows = P(("dp", "expert"), None)
    wide, tall = P("expert", None, "dp"), P("expert", "dp", None)
    return jax.shard_map(
        body,
        mesh=mesh,
        in_specs=(rows, rows, rows, wide, wide, tall, rows),
        out_specs=(rows, rows, wide, wide, tall),
        check_vma=False,
    )
```

```python
import functools

import jax
import jax.numpy as jnp
from jax import lax
from jax.experimental import pallas as pl
from jax.experimental.pallas import tpu as pltpu
from jax.sharding import PartitionSpec as P

BF = jnp.bfloat16
F32 = jnp.float32
NN = (((1,), (0,)), ((), ()))
NT = (((1,), (1,)), ((), ()))
TN = (((0,), (0,)), ((), ()))
MIB = 1024 * 1024
FLOPS_PER_US = 1153000000
VMEM = pl.BlockSpec(memory_space=pltpu.VMEM)
SMEM = pl.BlockSpec(memory_space=pltpu.SMEM)
HBM = pl.BlockSpec(memory_space=pltpu.HBM)
ANY = pl.BlockSpec(memory_space=pl.ANY)


def dot(a, b, dims=NN):
    return lax.dot_general(a, b, dims, preferred_element_type=F32)


def shaped(*shape):
    return jax.ShapeDtypeStruct(shape, BF)


TOKEN = shaped(16, 128)


def kernel_call(
    kernel, name, in_specs, out_specs, out_shape, scratch=(), limit=4, flops=0, alias=None, after=()
):
    count = len(in_specs)

    def run(*refs):
        kernel(*refs[:count], *refs[count + len(after) :])

    call = pl.pallas_call(
        run,
        in_specs=list(in_specs) + [ANY] * len(after),
        out_specs=out_specs,
        out_shape=out_shape,
        scratch_shapes=list(scratch),
        input_output_aliases=alias or {},
        cost_estimate=pl.CostEstimate(flops=flops, bytes_accessed=0, transcendentals=0),
        compiler_params=pltpu.CompilerParams(vmem_limit_bytes=limit * MIB),
        name=name,
    )
    return lambda *operands: call(*operands, *after)


def places(ids, experts):
    top, toks = ids.shape
    rows = lax.broadcasted_iota(jnp.int32, (experts, toks), 0)
    hot = [(ids[k : k + 1, :] == rows).astype(F32) for k in range(top)]
    earlier = (
        lax.broadcasted_iota(jnp.int32, (toks, toks), 0)
        < lax.broadcasted_iota(jnp.int32, (toks, toks), 1)
    ).astype(BF)
    counts = dot(sum(hot).astype(BF), earlier)
    return [jnp.sum(counts * h, axis=0, keepdims=True).astype(jnp.int32) for h in hot]


def start_all(pairs, sems):
    copies = [pltpu.make_async_copy(a, b, sems.at[i]) for i, (a, b) in enumerate(pairs)]
    for c in copies:
        c.start()
    return copies


def picks(ids, local, cap, experts, owner):
    top, toks = ids.shape
    here = places(ids, experts)
    rows = lax.broadcasted_iota(jnp.int32, (local * cap, toks), 0)
    return [
        jnp.where(
            (ids[k : k + 1, :] // local == owner)
            & ((ids[k : k + 1, :] % local) * cap + here[k] == rows),
            1.0,
            0.0,
        )
        for k in range(top)
    ]


def place_rows_kernel(experts, local, cap, expert_pos, ids_hbm, tok_hbm, out, chosen, *refs):
    ids_ref, tok_ref, sems = refs
    copies = start_all(((ids_hbm, ids_ref), (tok_hbm, tok_ref)), sems)
    copies[0].wait()
    ids = ids_ref[...]
    hits = []
    for j in range(experts // local):
        owner = jnp.bitwise_xor(expert_pos[0], j)
        hits.append(sum(picks(ids, local, cap, experts, owner)))
    chosen[...] = jnp.concatenate(hits, axis=0).astype(BF)
    copies[1].wait()
    out[...] = dot(chosen[...], tok_ref[...]).astype(BF)


def place_rows(expert_pos, ids, tokens, experts, local, cap):
    toks, width = tokens.shape
    return kernel_call(
        functools.partial(place_rows_kernel, experts, local, cap),
        "place_rows",
        [SMEM] + [HBM] * 2,
        [VMEM] * 2,
        [shaped(experts * cap, width), shaped(experts * cap, toks)],
        [pltpu.VMEM(a.shape, a.dtype) for a in (ids, tokens)] + [pltpu.SemaphoreType.DMA((2,))],
    )(expert_pos, ids, tokens)


def place_scaled_kernel(experts, local, cap, expert_pos, ids_hbm, gw_hbm, cot_hbm, *refs):
    out, high, low, ids_ref, gw_ref, cot_ref, sems = refs
    copies = start_all(((ids_hbm, ids_ref), (gw_hbm, gw_ref), (cot_hbm, cot_ref)), sems)
    copies[0].wait()
    copies[1].wait()
    ids = ids_ref[...]
    gw = gw_ref[...]
    hits, scales = [], []
    for j in range(experts // local):
        owner = jnp.bitwise_xor(expert_pos[0], j)
        hit = picks(ids, local, cap, experts, owner)
        hits.append(sum(hit))
        scales.append(sum(h * gw[k : k + 1, :] for k, h in enumerate(hit)))
    chosen = jnp.concatenate(hits, axis=0).astype(BF)
    scale = jnp.concatenate(scales, axis=0)
    high[...] = scale.astype(BF)
    low[...] = (scale - scale.astype(BF).astype(F32)).astype(BF)
    copies[2].wait()
    rows = dot(chosen, cot_ref[...])
    out[...] = (jnp.sum(scale, axis=1, keepdims=True) * rows).astype(BF)


def place_scaled(expert_pos, ids, gw, cot, experts, local, cap, after):
    toks, width = cot.shape
    return kernel_call(
        functools.partial(place_scaled_kernel, experts, local, cap),
        "place_scaled",
        [SMEM] + [HBM] * 3,
        [VMEM] * 3,
        [shaped(experts * cap, width)] + [shaped(experts * cap, toks)] * 2,
        [pltpu.VMEM(a.shape, a.dtype) for a in (ids, gw, cot)] + [pltpu.SemaphoreType.DMA((3,))],
        after=after,
    )(expert_pos, ids, gw, cot)


def blend_kernel(owners, cap, core, mine, theirs, *outs):
    size = mine.shape[0]
    part = size // owners
    row = lax.broadcasted_iota(jnp.int32, (size, size), 0)
    column = lax.broadcasted_iota(jnp.int32, (size, size), 1)
    first = core[0] * cap
    inside = row % part
    here = (inside >= first) & (inside < first + cap)
    shift = (1 - 2 * core[0]) * cap
    keep = jnp.where(here & (column == row), 1.0, 0.0).astype(BF)
    take = jnp.where((~here) & (column == row - shift), 1.0, 0.0).astype(BF)
    total = dot(keep, mine[...]) + dot(take, theirs[...])
    for j, out in enumerate(outs):
        out[...] = total[j * part : (j + 1) * part].astype(BF)


def blend(core, mine, theirs, owners, cap, after=()):
    size, width = mine.shape
    return kernel_call(
        functools.partial(blend_kernel, owners, cap),
        "blend",
        [SMEM] + [VMEM] * 2,
        [VMEM] * owners,
        [shaped(size // owners, width)] * owners,
        after=after,
    )(core, mine, theirs)


def join_kernel(*refs):
    parts, out = refs[:-1], refs[-1]
    out[...] = jnp.concatenate([p[...].astype(F32) for p in parts], axis=0).astype(BF)


def join(parts, after=(), flops=0):
    size, width = parts[0].shape
    return kernel_call(
        join_kernel,
        "join",
        [VMEM] * len(parts),
        VMEM,
        shaped(len(parts) * size, width),
        after=after,
        flops=flops,
    )(*parts)


def gather_rows(parts, out):
    first = 0
    for part in parts:
        out[first : first + part.shape[0], :] = part[...]
        first += part.shape[0]


def scatter_rows(total, parts, cols):
    first = 0
    for part in parts:
        part[:, cols] = total[first : first + part.shape[0]].astype(BF)
        first += part.shape[0]


def tile_of(hidden):
    return 256 if hidden % 256 == 0 else hidden


def chunks(total, size):
    return [slice(i, min(i + size, total)) for i in range(0, total, size)]


def forward_kernel(low, high, core, *refs):
    ps = refs[6:8]
    x, f1, f2, hid, gate_s, up_s = refs[8:]
    g0, u0, d0, g1, u1, d1 = (w.at[core[0]] for w in refs[:6])
    gather_rows((low, high), x)
    weights = ((g0, u0, d0), (g1, u1, d1))
    hidden = g0.shape[1]
    rows, width = x.shape
    turn = 0
    for half, (a, b, _) in enumerate(weights):
        for cols in chunks(hidden, tile_of(hidden)):
            gate_s[turn] = dot(x[...], a[:, cols])
            up_s[turn] = dot(x[...], b[:, cols])
            for r in chunks(rows, 64):
                gate, up = gate_s[turn, r], up_s[turn, r]
                sig = 1.0 / (1.0 + jnp.exp(-gate))
                act = gate * sig
                hid[half, r, cols] = (act * up).astype(BF)
                f1[half, r, cols] = (up * sig * (1.0 + gate * (1.0 - sig))).astype(BF)
                f2[half, r, cols] = act.astype(BF)
            turn = 1 - turn
    for cols in chunks(width, tile_of(width)):
        total = dot(hid[0], d0[:, cols]) + dot(hid[1], d1[:, cols])
        scatter_rows(total, ps, cols)


def forward(core, xs, own, other):
    size, width = xs[0].shape
    hidden = own[0].shape[2]
    rows = 2 * size
    out = kernel_call(
        forward_kernel,
        "forward",
        [VMEM] * 2 + [SMEM] + [VMEM] * 6,
        [VMEM] * 6,
        [shaped(size, width)] * 2 + [shaped(rows, width)] + [shaped(2, rows, hidden)] * 3,
        [pltpu.VMEM((2, rows, tile_of(hidden)), F32)] * 2,
        limit=32,
        flops=12 * rows * width * hidden,
    )(*xs, core, *own, *other)
    return out[:2], *out[2:]


def backward_kernel(low, high, core, *refs):
    f1, f2, qs = refs[6], refs[7], refs[8:10]
    dy, dg, du, da_s = refs[10:]
    g0, u0, d0, g1, u1, d1 = (w.at[core[0]] for w in refs[:6])
    gather_rows((low, high), dy)
    hidden = g0.shape[1]
    rows, width = dy.shape
    turn = 0
    for half, a in enumerate((d0, d1)):
        for cols in chunks(hidden, tile_of(hidden)):
            da_s[turn] = dot(dy[...], a[cols, :], NT)
            for r in chunks(rows, 64):
                da = da_s[turn, r]
                dg[half, r, cols] = (da * f1[half, r, cols].astype(F32)).astype(BF)
                du[half, r, cols] = (da * f2[half, r, cols].astype(F32)).astype(BF)
            turn = 1 - turn
    for cols in chunks(width, tile_of(width)):
        total = dot(dg[0], g0[cols, :], NT) + dot(du[0], u0[cols, :], NT)
        total = total + dot(dg[1], g1[cols, :], NT) + dot(du[1], u1[cols, :], NT)
        scatter_rows(total, qs, cols)


def backward(core, dys, own, other, f1, f2):
    size, width = dys[0].shape
    hidden = own[0].shape[2]
    rows = 2 * size
    out = kernel_call(
        backward_kernel,
        "backward",
        [VMEM] * 2 + [SMEM] + [VMEM] * 8,
        [VMEM] * 5,
        [shaped(size, width)] * 2 + [shaped(rows, width)] + [shaped(2, rows, hidden)] * 2,
        [pltpu.VMEM((2, rows, tile_of(hidden)), F32)],
        limit=32,
        flops=12 * rows * width * hidden,
    )(*dys, core, *own, *other, f1, f2)
    return out[:2], *out[2:]


def grads_kernel(half, core, x, dy, dg, du, hid, *refs):
    *refs, token = refs if half else (*refs[:3], *refs[4:], refs[3])
    token[...] = jnp.zeros(token.shape, BF)
    outs = [refs[0].at[i] for i in range(3)] if half else refs[3:6]
    hidden = dg.shape[2]
    width = x.shape[1]
    save = []

    def store(i):
        if not half:
            save.append(pltpu.make_async_copy(outs[i], refs[i].at[core[0]], refs[6].at[i]))
            save[i].start()

    for cols in chunks(hidden, tile_of(hidden)):
        outs[0][:, cols] = dot(x[...], dg[half, :, cols], TN).astype(BF)
    store(0)
    for cols in chunks(hidden, tile_of(hidden)):
        outs[1][:, cols] = dot(x[...], du[half, :, cols], TN).astype(BF)
    store(1)
    if half:
        for cols in chunks(hidden, tile_of(hidden)):
            outs[2][:, cols] = dot(dy[...], hid[half, :, cols], TN).astype(BF)
    else:
        for cols in chunks(width, tile_of(width)):
            outs[2][:, cols] = dot(hid[half], dy[:, cols], TN).astype(BF)
    store(2)
    for c in save:
        c.wait()


def grads(half, core, x, dy, dg, du, hid, local, after):
    rows, width = x.shape
    hidden = dg.shape[2]
    wide, tall = (width, hidden), (hidden, width)
    if half:
        outs, scratch = [shaped(3, *wide)], []
    else:
        outs = [shaped(local, *s) for s in (wide, wide, tall)]
        scratch = [pltpu.VMEM(s, BF) for s in (wide, wide, tall)] + [pltpu.SemaphoreType.DMA((3,))]
    return kernel_call(
        functools.partial(grads_kernel, half),
        "grads_given" if half else "grads_kept",
        [SMEM] + [VMEM] * 5,
        [VMEM if half else HBM] * len(outs) + [VMEM],
        outs + [TOKEN],
        scratch,
        limit=32,
        flops=6 * rows * width * hidden,
        after=after,
    )(core, x, dy, dg, du, hid)


def finish_kernel(core, got, *refs):
    outs, token, down, sems = refs[3:6], refs[6], refs[7], refs[8]
    token[...] = jnp.zeros(token.shape, BF)
    place = 1 - core[0]
    copies = start_all([(got.at[i], outs[i].at[place]) for i in range(2)], sems)
    down[...] = got[2].T
    copies += start_all([(down, outs[2].at[place])], sems.at[pl.ds(2, 1)])
    for c in copies:
        c.wait()


def finish(core, got, kept, after):
    return kernel_call(
        finish_kernel,
        "finish",
        [SMEM, VMEM] + [HBM] * 3,
        [HBM] * 3 + [VMEM],
        [shaped(*k.shape) for k in kept] + [TOKEN],
        [pltpu.VMEM(kept[2].shape[1:], BF), pltpu.SemaphoreType.DMA((3,))],
        limit=14,
        alias={2: 0, 3: 1, 4: 2},
        after=after,
    )(core, got, *kept)


def add_kernel(first, second, *outs):
    total = first[...].astype(F32) + second[...].astype(F32)
    size = total.shape[0] // len(outs)
    for j, out in enumerate(outs):
        out[...] = total[j * size : (j + 1) * size].astype(BF)


def add(arrays, pieces=1, after=()):
    rows, width = arrays[0].shape
    return kernel_call(
        add_kernel,
        "add",
        [VMEM] * 2,
        [VMEM] * pieces,
        [shaped(rows // pieces, width)] * pieces,
        after=after,
    )(*arrays)


def combine_kernel(weights, *refs):
    messages, out = refs[weights:-1], refs[-1]
    values = jnp.concatenate([m[...].astype(F32) for m in messages], axis=0).astype(BF)
    out[...] = sum(dot(w[...], values, TN) for w in refs[:weights]).astype(BF)


def combine(weights, messages, after=()):
    return kernel_call(
        functools.partial(combine_kernel, len(weights)),
        "combine",
        [VMEM] * (len(weights) + len(messages)),
        VMEM,
        shaped(weights[0].shape[1], messages[0].shape[1]),
        after=after,
    )(*weights, *messages)


def body(tokens, expert_ids, gate_weights, w_gate, w_up, w_down, cotangent):
    owners = lax.axis_size("expert")
    devices = lax.axis_size("dp")
    toks, width = tokens.shape
    top = expert_ids.shape[1]
    local = w_gate.shape[0]
    experts = local * owners
    cap = max(2, 5 * toks * top // (4 * experts))
    bits = (devices // 2).bit_length() - 1
    assert local == 2 and devices == 2 << bits and owners & (owners - 1) == 0

    side = lax.axis_index("dp") % 2
    core = side.astype(jnp.int32).reshape(1)
    expert_pos = lax.axis_index("expert").astype(jnp.int32).reshape(1)
    ids, gw = expert_ids.T, gate_weights.T

    def to_pair(a):
        return lax.ppermute(a, "dp", [(i, i ^ 1) for i in range(devices)])

    def to_owner(a, j):
        return lax.ppermute(a, "expert", [(i, i ^ j) for i in range(owners)])

    def to_chip(a, s):
        def bit(i):
            return 2 << ((s + (i % 2) * (bits // 2)) % bits)

        return lax.ppermute(a, "dp", [(i, i ^ bit(i)) for i in range(devices)])

    def swap(messages):
        return [messages[0]] + [to_owner(messages[j], j) for j in range(1, owners)]

    def widen(part, after=(), flops=0):
        for s in range(bits - 1):
            part = join([part, to_chip(part, s)], after, flops)
        return part

    def reduce(low, high, after=()):
        for s in reversed(range(1, bits)):
            low, high = add([low, to_chip(high, s)], 2, after)
        return low, high

    def hand_out(rows, after=()):
        return blend(core, rows, to_pair(rows), owners, cap, after)

    own = (w_gate, w_up, w_down)
    rows, chosen = place_rows(expert_pos, ids, tokens, experts, local, cap)
    messages = hand_out(rows)
    rows, high, low = place_scaled(expert_pos, ids, gw, cotangent, experts, local, cap, [rows])
    scaled = hand_out(rows)
    joined = join(swap(messages), scaled[:1])
    joined_scaled = join(swap(scaled), [joined], 18 * FLOPS_PER_US)
    x_low = widen(joined)
    x_high = to_chip(x_low, bits - 1)
    *behind, _ = lax.optimization_barrier((*own, x_low))
    other = [to_pair(w) for w in behind]
    dy_low = widen(joined_scaled, [x_low])
    dy_high = to_chip(dy_low, bits - 1)
    ps, x, f1, f2, hid = forward(core, (x_low, x_high), own, other)
    qs, dy, dg, du = backward(core, (dy_low, dy_high), own, other, f1, f2)
    p_low, p_high = reduce(*ps, [dy])
    given, token = grads(1, core, x, dy, dg, du, hid, local, [p_high])
    *kept, token = grads(0, core, x, dy, dg, du, hid, local, [token])
    q_low, q_high = reduce(*qs, [token])
    p_messages = hand_out(add([p_low, to_chip(p_high, 0)], 1, [q_high])[0])
    q_rows = add([q_low, to_chip(q_high, 0)], 1, p_messages[:1])[0]
    p_messages = swap(p_messages)
    early = join(p_messages[:-1], [q_rows], 20 * FLOPS_PER_US)
    q_messages = hand_out(q_rows, [early])
    p_messages = join(p_messages, q_messages[:1])
    mixed = combine([high, low], [p_messages], q_messages[:1])
    behind, _ = lax.optimization_barrier((given, q_messages[0]))
    got = to_pair(behind)
    grad_gate, grad_up, grad_down, token = finish(core, got, kept, [mixed])
    grad_tokens = combine([chosen], swap(q_messages), [token])
    return (mixed, grad_tokens, grad_gate, grad_up, grad_down)


def solution(mesh):
    rows = P(("dp", "expert"), None)
    wide, tall = P("expert", None, "dp"), P("expert", "dp", None)
    return jax.shard_map(
        body,
        mesh=mesh,
        in_specs=(rows, rows, rows, wide, wide, tall, rows),
        out_specs=(rows, rows, wide, wide, tall),
        check_vma=False,
    )
```

```python
import functools

import jax
import jax.numpy as jnp
from jax import lax
from jax.experimental import pallas as pl
from jax.experimental.pallas import tpu as pltpu
from jax.sharding import PartitionSpec as P

BF = jnp.bfloat16
F32 = jnp.float32
NN = (((1,), (0,)), ((), ()))
NT = (((1,), (1,)), ((), ()))
TN = (((0,), (0,)), ((), ()))
MIB = 1024 * 1024
FLOPS_PER_US = 1153000000
VMEM = pl.BlockSpec(memory_space=pltpu.VMEM)
SMEM = pl.BlockSpec(memory_space=pltpu.SMEM)
HBM = pl.BlockSpec(memory_space=pltpu.HBM)
ANY = pl.BlockSpec(memory_space=pl.ANY)


def dot(a, b, dims=NN):
    return lax.dot_general(a, b, dims, preferred_element_type=F32)


def shaped(*shape):
    return jax.ShapeDtypeStruct(shape, BF)


TOKEN = shaped(16, 128)


def kernel_call(
    kernel, name, in_specs, out_specs, out_shape, scratch=(), limit=4, flops=0, alias=None, after=()
):
    count = len(in_specs)

    def run(*refs):
        kernel(*refs[:count], *refs[count + len(after) :])

    call = pl.pallas_call(
        run,
        in_specs=list(in_specs) + [ANY] * len(after),
        out_specs=out_specs,
        out_shape=out_shape,
        scratch_shapes=list(scratch),
        input_output_aliases=alias or {},
        cost_estimate=pl.CostEstimate(flops=flops, bytes_accessed=0, transcendentals=0),
        compiler_params=pltpu.CompilerParams(vmem_limit_bytes=limit * MIB),
        name=name,
    )
    return lambda *operands: call(*operands, *after)


def places(ids, experts):
    top, toks = ids.shape
    rows = lax.broadcasted_iota(jnp.int32, (experts, toks), 0)
    hot = [(ids[k : k + 1, :] == rows).astype(F32) for k in range(top)]
    earlier = (
        lax.broadcasted_iota(jnp.int32, (toks, toks), 0)
        < lax.broadcasted_iota(jnp.int32, (toks, toks), 1)
    ).astype(BF)
    counts = dot(sum(hot).astype(BF), earlier)
    return [jnp.sum(counts * h, axis=0, keepdims=True).astype(jnp.int32) for h in hot]


def start_all(pairs, sems):
    copies = [pltpu.make_async_copy(a, b, sems.at[i]) for i, (a, b) in enumerate(pairs)]
    for c in copies:
        c.start()
    return copies


def picks(ids, local, cap, experts, owner):
    top, toks = ids.shape
    here = places(ids, experts)
    rows = lax.broadcasted_iota(jnp.int32, (local * cap, toks), 0)
    return [
        jnp.where(
            (ids[k : k + 1, :] // local == owner)
            & ((ids[k : k + 1, :] % local) * cap + here[k] == rows),
            1.0,
            0.0,
        )
        for k in range(top)
    ]


def place_rows_kernel(experts, local, cap, expert_pos, ids_hbm, tok_hbm, out, chosen, *refs):
    ids_ref, tok_ref, sems = refs
    copies = start_all(((ids_hbm, ids_ref), (tok_hbm, tok_ref)), sems)
    copies[0].wait()
    ids = ids_ref[...]
    hits = []
    for j in range(experts // local):
        owner = jnp.bitwise_xor(expert_pos[0], j)
        hits.append(sum(picks(ids, local, cap, experts, owner)))
    chosen[...] = jnp.concatenate(hits, axis=0).astype(BF)
    copies[1].wait()
    out[...] = dot(chosen[...], tok_ref[...]).astype(BF)


def place_rows(expert_pos, ids, tokens, experts, local, cap):
    toks, width = tokens.shape
    return kernel_call(
        functools.partial(place_rows_kernel, experts, local, cap),
        "place_rows",
        [SMEM] + [HBM] * 2,
        [VMEM] * 2,
        [shaped(experts * cap, width), shaped(experts * cap, toks)],
        [pltpu.VMEM(a.shape, a.dtype) for a in (ids, tokens)] + [pltpu.SemaphoreType.DMA((2,))],
    )(expert_pos, ids, tokens)


def place_scaled_kernel(experts, local, cap, expert_pos, ids_hbm, gw_hbm, cot_hbm, *refs):
    out, high, low, ids_ref, gw_ref, cot_ref, sems = refs
    copies = start_all(((ids_hbm, ids_ref), (gw_hbm, gw_ref), (cot_hbm, cot_ref)), sems)
    copies[0].wait()
    copies[1].wait()
    ids = ids_ref[...]
    gw = gw_ref[...]
    hits, scales = [], []
    for j in range(experts // local):
        owner = jnp.bitwise_xor(expert_pos[0], j)
        hit = picks(ids, local, cap, experts, owner)
        hits.append(sum(hit))
        scales.append(sum(h * gw[k : k + 1, :] for k, h in enumerate(hit)))
    chosen = jnp.concatenate(hits, axis=0).astype(BF)
    scale = jnp.concatenate(scales, axis=0)
    high[...] = scale.astype(BF)
    low[...] = (scale - scale.astype(BF).astype(F32)).astype(BF)
    copies[2].wait()
    rows = dot(chosen, cot_ref[...])
    out[...] = (jnp.sum(scale, axis=1, keepdims=True) * rows).astype(BF)


def place_scaled(expert_pos, ids, gw, cot, experts, local, cap, after):
    toks, width = cot.shape
    return kernel_call(
        functools.partial(place_scaled_kernel, experts, local, cap),
        "place_scaled",
        [SMEM] + [HBM] * 3,
        [VMEM] * 3,
        [shaped(experts * cap, width)] + [shaped(experts * cap, toks)] * 2,
        [pltpu.VMEM(a.shape, a.dtype) for a in (ids, gw, cot)] + [pltpu.SemaphoreType.DMA((3,))],
        after=after,
    )(expert_pos, ids, gw, cot)


def blend_kernel(owners, cap, core, mine, theirs, *outs):
    size = mine.shape[0]
    part = size // owners
    row = lax.broadcasted_iota(jnp.int32, (size, size), 0)
    column = lax.broadcasted_iota(jnp.int32, (size, size), 1)
    first = core[0] * cap
    inside = row % part
    here = (inside >= first) & (inside < first + cap)
    shift = (1 - 2 * core[0]) * cap
    keep = jnp.where(here & (column == row), 1.0, 0.0).astype(BF)
    take = jnp.where((~here) & (column == row - shift), 1.0, 0.0).astype(BF)
    total = dot(keep, mine[...]) + dot(take, theirs[...])
    for j, out in enumerate(outs):
        out[...] = total[j * part : (j + 1) * part].astype(BF)


def blend(core, mine, theirs, owners, cap, after=()):
    size, width = mine.shape
    return kernel_call(
        functools.partial(blend_kernel, owners, cap),
        "blend",
        [SMEM] + [VMEM] * 2,
        [VMEM] * owners,
        [shaped(size // owners, width)] * owners,
        after=after,
    )(core, mine, theirs)


def join_kernel(*refs):
    parts, out = refs[:-1], refs[-1]
    out[...] = jnp.concatenate([p[...].astype(F32) for p in parts], axis=0).astype(BF)


def join(parts, after=(), flops=0):
    size, width = parts[0].shape
    return kernel_call(
        join_kernel,
        "join",
        [VMEM] * len(parts),
        VMEM,
        shaped(len(parts) * size, width),
        after=after,
        flops=flops,
    )(*parts)


def gather_rows(parts, out):
    first = 0
    for part in parts:
        out[first : first + part.shape[0], :] = part[...]
        first += part.shape[0]


def scatter_rows(total, parts, cols):
    first = 0
    for part in parts:
        part[:, cols] = total[first : first + part.shape[0]].astype(BF)
        first += part.shape[0]


def tile_of(hidden):
    return 256 if hidden % 256 == 0 else hidden


def chunks(total, size):
    return [slice(i, min(i + size, total)) for i in range(0, total, size)]


def forward_kernel(low, high, core, *refs):
    ps = refs[6:8]
    x, f1, f2, hid, gate_s, up_s = refs[8:]
    g0, u0, d0, g1, u1, d1 = (w.at[core[0]] for w in refs[:6])
    gather_rows((low, high), x)
    weights = ((g0, u0, d0), (g1, u1, d1))
    hidden = g0.shape[1]
    rows, width = x.shape
    turn = 0
    for half, (a, b, _) in enumerate(weights):
        for cols in chunks(hidden, tile_of(hidden)):
            gate_s[turn] = dot(x[...], a[:, cols])
            up_s[turn] = dot(x[...], b[:, cols])
            for r in chunks(rows, 64):
                gate, up = gate_s[turn, r], up_s[turn, r]
                sig = 1.0 / (1.0 + jnp.exp(-gate))
                act = gate * sig
                hid[half, r, cols] = (act * up).astype(BF)
                f1[half, r, cols] = (up * sig * (1.0 + gate * (1.0 - sig))).astype(BF)
                f2[half, r, cols] = act.astype(BF)
            turn = 1 - turn
    for cols in chunks(width, tile_of(width)):
        total = dot(hid[0], d0[:, cols]) + dot(hid[1], d1[:, cols])
        scatter_rows(total, ps, cols)


def forward(core, xs, own, other):
    size, width = xs[0].shape
    hidden = own[0].shape[2]
    rows = 2 * size
    out = kernel_call(
        forward_kernel,
        "forward",
        [VMEM] * 2 + [SMEM] + [VMEM] * 6,
        [VMEM] * 6,
        [shaped(size, width)] * 2 + [shaped(rows, width)] + [shaped(2, rows, hidden)] * 3,
        [pltpu.VMEM((2, rows, tile_of(hidden)), F32)] * 2,
        limit=32,
        flops=12 * rows * width * hidden,
    )(*xs, core, *own, *other)
    return out[:2], *out[2:]


def backward_kernel(low, high, core, *refs):
    f1, f2, qs = refs[6], refs[7], refs[8:10]
    dy, dg, du, da_s = refs[10:]
    g0, u0, d0, g1, u1, d1 = (w.at[core[0]] for w in refs[:6])
    gather_rows((low, high), dy)
    hidden = g0.shape[1]
    rows, width = dy.shape
    turn = 0
    for half, a in enumerate((d0, d1)):
        for cols in chunks(hidden, tile_of(hidden)):
            da_s[turn] = dot(dy[...], a[cols, :], NT)
            for r in chunks(rows, 64):
                da = da_s[turn, r]
                dg[half, r, cols] = (da * f1[half, r, cols].astype(F32)).astype(BF)
                du[half, r, cols] = (da * f2[half, r, cols].astype(F32)).astype(BF)
            turn = 1 - turn
    for cols in chunks(width, tile_of(width)):
        total = dot(dg[0], g0[cols, :], NT) + dot(du[0], u0[cols, :], NT)
        total = total + dot(dg[1], g1[cols, :], NT) + dot(du[1], u1[cols, :], NT)
        scatter_rows(total, qs, cols)


def backward(core, dys, own, other, f1, f2):
    size, width = dys[0].shape
    hidden = own[0].shape[2]
    rows = 2 * size
    out = kernel_call(
        backward_kernel,
        "backward",
        [VMEM] * 2 + [SMEM] + [VMEM] * 8,
        [VMEM] * 5,
        [shaped(size, width)] * 2 + [shaped(rows, width)] + [shaped(2, rows, hidden)] * 2,
        [pltpu.VMEM((2, rows, tile_of(hidden)), F32)],
        limit=32,
        flops=12 * rows * width * hidden,
    )(*dys, core, *own, *other, f1, f2)
    return out[:2], *out[2:]


def grads_kernel(half, core, x, dy, dg, du, hid, *refs):
    *refs, token = refs if half else (*refs[:3], *refs[4:], refs[3])
    token[...] = jnp.zeros(token.shape, BF)
    outs = [refs[0].at[i] for i in range(3)] if half else refs[3:6]
    hidden = dg.shape[2]
    width = x.shape[1]
    save = []

    def store(i):
        if not half:
            save.append(pltpu.make_async_copy(outs[i], refs[i].at[core[0]], refs[6].at[i]))
            save[i].start()

    for cols in chunks(hidden, tile_of(hidden)):
        outs[0][:, cols] = dot(x[...], dg[half, :, cols], TN).astype(BF)
    store(0)
    for cols in chunks(hidden, tile_of(hidden)):
        outs[1][:, cols] = dot(x[...], du[half, :, cols], TN).astype(BF)
    store(1)
    if half:
        for cols in chunks(hidden, tile_of(hidden)):
            outs[2][:, cols] = dot(dy[...], hid[half, :, cols], TN).astype(BF)
    else:
        for cols in chunks(width, tile_of(width)):
            outs[2][:, cols] = dot(hid[half], dy[:, cols], TN).astype(BF)
    store(2)
    for c in save:
        c.wait()


def grads(half, core, x, dy, dg, du, hid, local, after):
    rows, width = x.shape
    hidden = dg.shape[2]
    wide, tall = (width, hidden), (hidden, width)
    if half:
        outs, scratch = [shaped(3, *wide)], []
    else:
        outs = [shaped(local, *s) for s in (wide, wide, tall)]
        scratch = [pltpu.VMEM(s, BF) for s in (wide, wide, tall)] + [pltpu.SemaphoreType.DMA((3,))]
    return kernel_call(
        functools.partial(grads_kernel, half),
        "grads_given" if half else "grads_kept",
        [SMEM] + [VMEM] * 5,
        [VMEM if half else HBM] * len(outs) + [VMEM],
        outs + [TOKEN],
        scratch,
        limit=32,
        flops=6 * rows * width * hidden,
        after=after,
    )(core, x, dy, dg, du, hid)


def finish_kernel(core, got, *refs):
    outs, token, down, sems = refs[3:6], refs[6], refs[7], refs[8]
    token[...] = jnp.zeros(token.shape, BF)
    place = 1 - core[0]
    copies = start_all([(got.at[i], outs[i].at[place]) for i in range(2)], sems)
    down[...] = got[2].T
    copies += start_all([(down, outs[2].at[place])], sems.at[pl.ds(2, 1)])
    for c in copies:
        c.wait()


def finish(core, got, kept, after):
    return kernel_call(
        finish_kernel,
        "finish",
        [SMEM, VMEM] + [HBM] * 3,
        [HBM] * 3 + [VMEM],
        [shaped(*k.shape) for k in kept] + [TOKEN],
        [pltpu.VMEM(kept[2].shape[1:], BF), pltpu.SemaphoreType.DMA((3,))],
        limit=14,
        alias={2: 0, 3: 1, 4: 2},
        after=after,
    )(core, got, *kept)


def add_kernel(first, second, *outs):
    total = first[...].astype(F32) + second[...].astype(F32)
    size = total.shape[0] // len(outs)
    for j, out in enumerate(outs):
        out[...] = total[j * size : (j + 1) * size].astype(BF)


def add(arrays, pieces=1, after=()):
    rows, width = arrays[0].shape
    return kernel_call(
        add_kernel,
        "add",
        [VMEM] * 2,
        [VMEM] * pieces,
        [shaped(rows // pieces, width)] * pieces,
        after=after,
    )(*arrays)


def combine_kernel(weights, *refs):
    messages, out = refs[weights:-1], refs[-1]
    values = jnp.concatenate([m[...].astype(F32) for m in messages], axis=0).astype(BF)
    out[...] = sum(dot(w[...], values, TN) for w in refs[:weights]).astype(BF)


def combine(weights, messages, after=()):
    return kernel_call(
        functools.partial(combine_kernel, len(weights)),
        "combine",
        [VMEM] * (len(weights) + len(messages)),
        VMEM,
        shaped(weights[0].shape[1], messages[0].shape[1]),
        after=after,
    )(*weights, *messages)


def combine_both_kernel(high, low, chosen, *refs):
    count = (len(refs) - 2) // 2
    first, second = [
        jnp.concatenate([m[...].astype(F32) for m in part], axis=0).astype(BF)
        for part in (refs[:count], refs[count : 2 * count])
    ]
    refs[-2][...] = (dot(high[...], first, TN) + dot(low[...], first, TN)).astype(BF)
    refs[-1][...] = dot(chosen[...], second, TN).astype(BF)


def combine_both(weights, first, second, after):
    out = shaped(weights[0].shape[1], first[0].shape[1])
    return kernel_call(
        combine_both_kernel,
        "combine_both",
        [VMEM] * (3 + len(first) + len(second)),
        [VMEM] * 2,
        [out] * 2,
        after=after,
    )(*weights, *first, *second)


def body(tokens, expert_ids, gate_weights, w_gate, w_up, w_down, cotangent):
    owners = lax.axis_size("expert")
    devices = lax.axis_size("dp")
    toks, width = tokens.shape
    top = expert_ids.shape[1]
    local = w_gate.shape[0]
    experts = local * owners
    cap = max(2, 5 * toks * top // (4 * experts))
    bits = (devices // 2).bit_length() - 1
    assert local == 2 and devices == 2 << bits and owners & (owners - 1) == 0

    side = lax.axis_index("dp") % 2
    core = side.astype(jnp.int32).reshape(1)
    expert_pos = lax.axis_index("expert").astype(jnp.int32).reshape(1)
    ids, gw = expert_ids.T, gate_weights.T

    def to_pair(a):
        return lax.ppermute(a, "dp", [(i, i ^ 1) for i in range(devices)])

    def to_owner(a, j):
        return lax.ppermute(a, "expert", [(i, i ^ j) for i in range(owners)])

    def to_chip(a, s):
        def bit(i):
            return 2 << ((s + (i % 2) * (bits // 2)) % bits)

        return lax.ppermute(a, "dp", [(i, i ^ bit(i)) for i in range(devices)])

    def swap(messages):
        return [messages[0]] + [to_owner(messages[j], j) for j in range(1, owners)]

    def widen(part, after=(), flops=0):
        for s in range(bits - 1):
            part = join([part, to_chip(part, s)], after, flops)
        return part

    def reduce(low, high, after=()):
        for s in reversed(range(1, bits)):
            low, high = add([low, to_chip(high, s)], 2, after)
        return low, high

    def hand_out(rows, after=()):
        return blend(core, rows, to_pair(rows), owners, cap, after)

    own = (w_gate, w_up, w_down)
    rows, chosen = place_rows(expert_pos, ids, tokens, experts, local, cap)
    messages = hand_out(rows)
    rows, high, low = place_scaled(expert_pos, ids, gw, cotangent, experts, local, cap, [rows])
    scaled = hand_out(rows)
    joined = join(swap(messages), scaled[:1])
    joined_scaled = join(swap(scaled), [joined], 18 * FLOPS_PER_US)
    x_low = widen(joined)
    x_high = to_chip(x_low, bits - 1)
    *behind, _ = lax.optimization_barrier((*own, x_low))
    other = [to_pair(w) for w in behind]
    dy_low = widen(joined_scaled, [x_low])
    dy_high = to_chip(dy_low, bits - 1)
    ps, x, f1, f2, hid = forward(core, (x_low, x_high), own, other)
    qs, dy, dg, du = backward(core, (dy_low, dy_high), own, other, f1, f2)
    p_low, p_high = reduce(*ps, [dy])
    given, token = grads(1, core, x, dy, dg, du, hid, local, [p_high])
    *kept, token = grads(0, core, x, dy, dg, du, hid, local, [token])
    q_low, q_high = reduce(*qs, [token])
    p_messages = hand_out(add([p_low, to_chip(p_high, 0)], 1, [q_high])[0])
    q_rows = add([q_low, to_chip(q_high, 0)], 1, p_messages[:1])[0]
    p_messages = swap(p_messages)
    early = join(p_messages[:-1], [q_rows], 20 * FLOPS_PER_US)
    q_messages = hand_out(q_rows, [early])
    behind, _ = lax.optimization_barrier((given, q_messages[0]))
    got = to_pair(behind)
    grad_gate, grad_up, grad_down, token = finish(core, got, kept, q_messages[:1])
    mixed, grad_tokens = combine_both([high, low, chosen], p_messages, swap(q_messages), [token])
    return (mixed, grad_tokens, grad_gate, grad_up, grad_down)


def solution(mesh):
    rows = P(("dp", "expert"), None)
    wide, tall = P("expert", None, "dp"), P("expert", "dp", None)
    return jax.shard_map(
        body,
        mesh=mesh,
        in_specs=(rows, rows, rows, wide, wide, tall, rows),
        out_specs=(rows, rows, wide, wide, tall),
        check_vma=False,
    )
```
